32 devices in a mesh: group: 2 (over x), fsdp: 4 (over y, core), tensor: 4 (over z).
Axes of the slice: x: 2, y: 2, z: 4, core: 2. Of those that a mesh axis runs over, the one named last changes fastest.
Arguments:
- tokens: bfloat16 [2048, 4096], P(('group', 'fsdp'), 'tensor'), parts along dimension 0, may hold values from -6 to 6
- cotangent: bfloat16 [2048, 4096], P(('group', 'fsdp'), 'tensor'), parts along dimension 0, may hold values from -6 to 6
- gate_blocks: bfloat16 [4, 12, 128, 128], P('tensor', 'fsdp'), may hold values from -1 to 1
- up_blocks: bfloat16 [4, 12, 128, 128], P('tensor', 'fsdp'), may hold values from -1 to 1
- down_blocks: bfloat16 [4, 12, 128, 128], P('tensor', 'fsdp'), may hold values from -0.5 to 0.5
- block_rows: int32 [3, 4, 12], P(None, 'tensor'), may hold values from 0 to 31, as said below
- col_counts: int32 [3, 4, 28], P(None, 'tensor'), may hold values from 0 to 12, as said below
Outputs:
- layer_out: bfloat16 [2048, 4096], P(('group', 'fsdp'), 'tensor'), parts along dimension 0
- input_grad: bfloat16 [2048, 4096], P(('group', 'fsdp'), 'tensor'), parts along dimension 0
- gate_grad: bfloat16 [8, 12, 128, 128], P(('group', 'tensor'), 'fsdp'), parts along dimension 0
- up_grad: bfloat16 [8, 12, 128, 128], P(('group', 'tensor'), 'fsdp'), parts along dimension 0
- down_grad: bfloat16 [8, 12, 128, 128], P(('group', 'tensor'), 'fsdp'), parts along dimension 0
The draws below stay inside these ranges and needn't reach their ends.
There are 2 independent parts, one for each index of `group`. The reference program is written for one: setup_inputs(seed, part) draws one part's arguments, and reference() takes and returns one part's arrays. A program takes and returns all parts, laid end to end along the dimension named above; an argument that names none is the same for every part. Nothing has to cross between parts.
Inputs may be any that keep to these rules, and one draw needn't show every extreme that they name: `block_rows`: for each matrix and tensor index, the live slots list their blocks column by column, feature blocks ascending within a column and no block twice; the entries past the live ones are 0. `col_counts`: for each matrix and tensor index the counts sum to half of 12 or more and to at most 12, and to exactly 12 at one tensor index of each matrix.
All inputs are finite; a program needn't handle non-finite values.
Results may differ from the reference program's by a relative error of at most 0.011.
Values may be sent and summed in bfloat16 or wider, within the bound.
A program may use at most 128 MiB of HBM per device.

```python
import jax
import jax.numpy as jnp
from jax import lax

D = 4096
BLK = 128
TOKENS = 1024
NBD = 32
CPR = 28
SLOTS = 12
N_FSDP = 4
N_TENSOR = 4


def mask_tables(key):
    total_places = NBD * CPR
    key_lives, key_busy, key_order = jax.random.split(key, 3)
    live_counts = jax.random.randint(key_lives, (3, N_TENSOR), SLOTS // 2, SLOTS + 1)
    busiest = jax.random.randint(key_busy, (3, 1), 0, N_TENSOR)
    tensor_ids = jnp.arange(N_TENSOR, dtype=jnp.int32)[None, :]
    is_busiest = tensor_ids == busiest
    live_counts = jnp.where(is_busiest, SLOTS, live_counts)
    order_keys = jax.random.split(key_order, 3 * N_TENSOR)

    def shuffled_one(one_key):
        return jax.random.permutation(one_key, total_places)
    shuffled = jax.vmap(shuffled_one)(order_keys).reshape(3, N_TENSOR, total_places)
    places = jnp.arange(total_places, dtype=jnp.int32)
    first_column = (places < NBD)[None, None, :]
    forced = is_busiest[:, :, None] & first_column
    chosen = (shuffled < live_counts[:, :, None]) | forced
    scores = jnp.where(chosen, places, total_places + places)
    picked = jnp.argsort(scores, axis=-1, stable=True)[:, :, :SLOTS].astype(jnp.int32)
    slot_ids = jnp.arange(SLOTS, dtype=jnp.int32)
    is_live = slot_ids[None, None, :] < live_counts[:, :, None]
    slot_rows = jnp.where(is_live, picked % NBD, 0).astype(jnp.int32)
    columns = picked // NBD
    column_ids = jnp.arange(CPR, dtype=jnp.int32)
    counts = jnp.sum((is_live[..., None] & (columns[..., None] == column_ids)).astype(jnp.int32), axis=2)
    return (slot_rows, counts.astype(jnp.int32))


def draw_block_rows(key, part):
    return mask_tables(key)[0]


def draw_col_counts(key, part):
    return mask_tables(key)[1]


def block_levels(rng, dims, cuts, low, largest):
    factor_of = 1.0
    for position, blocks in cuts:
        heights = jax.random.uniform(jax.random.fold_in(jax.random.fold_in(rng, 6), position), (blocks,), jnp.float32, low / len(cuts), largest / len(cuts))
        factor_of = factor_of * jnp.repeat(jnp.exp(heights), dims[position] // blocks).reshape((-1,) + (1,) * (len(dims) - 1 - position))
    return factor_of


def normal_values(key, extent, spread, most, cuts=(), kind=jnp.bfloat16):
    drawn = jax.random.normal(key, extent, jnp.float32) * spread
    if len(cuts) > 0:
        drawn = block_levels(key, extent, cuts, -0.22, 0.18) * drawn
    return jnp.clip(drawn, min=-most, max=most).astype(kind)


def setup_inputs(seed: int = 0, part: int = 0) -> dict:
    key_list = jax.random.split(jax.random.key(seed), 8)
    own_keys = jax.random.split(jax.random.fold_in(key_list[7], part), 8)
    return {
        "tokens": normal_values(own_keys[0], (TOKENS, D), 1.0, 6.0, ((0, 4), (1, 4))),
        "cotangent": normal_values(own_keys[1], (TOKENS, D), 1.0, 6.0, ((0, 4), (1, 4))),
        "gate_blocks": normal_values(key_list[2], (N_TENSOR, SLOTS, BLK, BLK), (3 * SLOTS * BLK // (4 * CPR)) ** -0.5, 1.0, ((0, 4), (1, 4))),
        "up_blocks": normal_values(key_list[3], (N_TENSOR, SLOTS, BLK, BLK), (3 * SLOTS * BLK // (4 * CPR)) ** -0.5, 1.0, ((0, 4), (1, 4))),
        "down_blocks": normal_values(key_list[4], (N_TENSOR, SLOTS, BLK, BLK), (3 * SLOTS * BLK * N_TENSOR // (4 * NBD)) ** -0.5, 0.5, ((0, 4), (1, 4))),
        "block_rows": draw_block_rows(jax.random.fold_in(key_list[7], 71), part),
        "col_counts": draw_col_counts(jax.random.fold_in(key_list[7], 71), part),
    }


finest = lax.Precision.HIGHEST

def slot_columns(counts, slot_count):
    running = jnp.cumsum(counts)
    places = lax.broadcasted_iota(jnp.int32, (slot_count, counts.shape[0]), 0)
    return lax.optimization_barrier(jnp.sum((running[None, :] <= places).astype(jnp.int32), axis=1))

def slot_tables(slot_rows, counts, feature_count):
    slot_count = slot_rows.shape[0]
    col_width = counts.shape[0]
    columns = slot_columns(counts, slot_count)
    col_hot = (columns[:, None] == lax.broadcasted_iota(jnp.int32, (slot_count, col_width), 1)).astype(jnp.float32)
    row_hot = (slot_rows[:, None] == lax.broadcasted_iota(jnp.int32, (slot_count, feature_count), 1)).astype(jnp.float32)
    is_live = columns < col_width
    picker = jnp.minimum(columns, col_width - 1)
    return (col_hot, row_hot, is_live, picker)

def into_columns(terms, col_hot):
    return jnp.einsum('tsn,sc->tcn', terms, col_hot, precision=finest)

def into_rows(terms, row_hot):
    return jnp.einsum('tsk,sr->trk', terms, row_hot, precision=finest)

def pick_columns(values, picker, is_live):
    chosen = jnp.take(values, picker, axis=1)
    return jnp.where(is_live[None, :, None], chosen, jnp.zeros_like(chosen))

def as_float(values):
    return values.astype(jnp.float32)

def group_grad(left_side, right_side):
    tok_count = left_side.shape[0]
    left_side = left_side.reshape(N_FSDP, tok_count // N_FSDP, left_side.shape[1], left_side.shape[2])
    right_side = right_side.reshape(N_FSDP, tok_count // N_FSDP, right_side.shape[1], right_side.shape[2])
    partial_sums = jnp.einsum('ftsa,ftsb->fsab', as_float(left_side), as_float(right_side), precision=finest)
    rounded = lax.optimization_barrier(partial_sums.astype(jnp.bfloat16))
    return lax.optimization_barrier(jnp.sum(rounded.astype(jnp.float32), axis=0)).astype(jnp.bfloat16)

def rank_terms(tokens, cotangent, gate_w, up_w, down_w, slot_rows, counts):
    tok_count = tokens.shape[0]
    side = gate_w.shape[-1]
    feature_count = tokens.shape[1] // side
    token_blocks = tokens.reshape(tok_count, feature_count, side)
    grad_blocks = cotangent.reshape(tok_count, feature_count, side)
    gate_tab = slot_tables(slot_rows[0], counts[0], feature_count)
    up_tab = slot_tables(slot_rows[1], counts[1], feature_count)
    down_tab = slot_tables(slot_rows[2], counts[2], feature_count)
    gate_in = jnp.take(token_blocks, slot_rows[0], axis=1)
    up_in = jnp.take(token_blocks, slot_rows[1], axis=1)
    gate_pre = into_columns(jnp.einsum('tsk,skn->tsn', as_float(gate_in), as_float(gate_w), precision=finest), gate_tab[0])
    up_pre = into_columns(jnp.einsum('tsk,skn->tsn', as_float(up_in), as_float(up_w), precision=finest), up_tab[0])
    sigma_gate = jax.nn.sigmoid(gate_pre)
    active = gate_pre * sigma_gate
    hidden = (active * up_pre).astype(jnp.bfloat16)
    down_in = pick_columns(hidden, down_tab[3], down_tab[2])
    out_terms = jnp.einsum('tsn,snk->tsk', as_float(down_in), as_float(down_w), precision=finest)
    out_part = into_rows(out_terms, down_tab[1]).reshape(tok_count, -1)
    down_back = jnp.take(grad_blocks, slot_rows[2], axis=1)
    back_terms = jnp.einsum('tsk,snk->tsn', as_float(down_back), as_float(down_w), precision=finest)
    dhidden = into_columns(back_terms, down_tab[0])
    dgate = (dhidden * up_pre * sigma_gate * (1.0 + gate_pre * (1.0 - sigma_gate))).astype(jnp.bfloat16)
    dup = (dhidden * active).astype(jnp.bfloat16)
    gate_back = pick_columns(dgate, gate_tab[3], gate_tab[2])
    up_back = pick_columns(dup, up_tab[3], up_tab[2])
    gate_terms = jnp.einsum('tsn,skn->tsk', as_float(gate_back), as_float(gate_w), precision=finest)
    up_terms = jnp.einsum('tsn,skn->tsk', as_float(up_back), as_float(up_w), precision=finest)
    in_part = (into_rows(gate_terms, gate_tab[1]) + into_rows(up_terms, up_tab[1])).reshape(tok_count, -1)
    gate_grad = group_grad(gate_in, gate_back)
    up_grad = group_grad(up_in, up_back)
    down_grad = group_grad(down_in, down_back)
    return (out_part, in_part, gate_grad, up_grad, down_grad)

def add_rounded(parts):
    rounded = lax.optimization_barrier(parts.astype(jnp.bfloat16))
    return lax.optimization_barrier(jnp.sum(rounded.astype(jnp.float32), axis=0)).astype(jnp.bfloat16)

def reference(tokens, cotangent, gate_blocks, up_blocks, down_blocks, block_rows, col_counts):

    def one_rank(items):
        gate_w, up_w, down_w, slot_rows, counts = items
        return rank_terms(tokens, cotangent, gate_w, up_w, down_w, slot_rows, counts)
    out_parts, in_parts, gate_grad, up_grad, down_grad = lax.map(one_rank, (gate_blocks, up_blocks, down_blocks, jnp.swapaxes(block_rows, 0, 1), jnp.swapaxes(col_counts, 0, 1)))
    return (add_rounded(out_parts), add_rounded(in_parts), gate_grad, up_grad, down_grad)
```

```python
import functools

import jax
import jax.numpy as jnp
from jax import lax
from jax.experimental import pallas as pl
from jax.experimental.pallas import tpu as pltpu
from jax.sharding import PartitionSpec as P

finest = lax.Precision.HIGHEST


def slot_columns(counts, slot_count):
    running = jnp.cumsum(counts)
    places = lax.broadcasted_iota(jnp.int32, (slot_count, counts.shape[0]), 0)
    return jnp.sum((running[None, :] <= places).astype(jnp.int32), axis=1)


def slot_tables(slot_rows, counts, feature_count):
    slot_count = slot_rows.shape[0]
    col_width = counts.shape[0]
    columns = slot_columns(counts, slot_count)
    col_hot = (
        columns[:, None] == lax.broadcasted_iota(jnp.int32, (slot_count, col_width), 1)
    ).astype(jnp.float32)
    row_hot = (
        slot_rows[:, None] == lax.broadcasted_iota(jnp.int32, (slot_count, feature_count), 1)
    ).astype(jnp.float32)
    is_live = columns < col_width
    picker = jnp.minimum(columns, col_width - 1)
    return (col_hot, row_hot, is_live, picker)


def into_columns(terms, col_hot):
    return jnp.einsum("tsn,sc->tcn", terms, col_hot, precision=finest)


def into_rows(terms, row_hot):
    return jnp.einsum("tsk,sr->trk", terms, row_hot, precision=finest)


def pick_columns(values, picker, is_live):
    chosen = jnp.take(values, picker, axis=1)
    return jnp.where(is_live[None, :, None], chosen, jnp.zeros_like(chosen))


def gathered_plan(tokens, cotangent, gate_blocks, up_blocks, down_blocks, block_rows, col_counts):
    full_tokens = lax.all_gather(tokens, "tensor", axis=1, tiled=True)
    gate_w, up_w = (
        lax.all_gather(gate_blocks[0], "fsdp", axis=0, tiled=True),
        lax.all_gather(up_blocks[0], "fsdp", axis=0, tiled=True),
    )
    slot_rows = block_rows[:, 0, :]
    counts = col_counts[:, 0, :]
    tok_count = full_tokens.shape[0]
    side = gate_w.shape[-1]
    feature_count = full_tokens.shape[1] // side
    token_blocks = full_tokens.reshape(tok_count, feature_count, side)
    gate_tab = slot_tables(slot_rows[0], counts[0], feature_count)
    up_tab = slot_tables(slot_rows[1], counts[1], feature_count)
    down_tab = slot_tables(slot_rows[2], counts[2], feature_count)
    gate_in = jnp.take(token_blocks, slot_rows[0], axis=1)
    up_in = jnp.take(token_blocks, slot_rows[1], axis=1)
    gate_pre = into_columns(
        jnp.einsum("tsk,skn->tsn", gate_in, gate_w, preferred_element_type=jnp.float32), gate_tab[0]
    )
    up_pre = into_columns(
        jnp.einsum("tsk,skn->tsn", up_in, up_w, preferred_element_type=jnp.float32), up_tab[0]
    )
    sigma_gate = jax.nn.sigmoid(gate_pre)
    active = gate_pre * sigma_gate
    hidden = (active * up_pre).astype(jnp.bfloat16)
    down_w = lax.all_gather(down_blocks[0], "fsdp", axis=0, tiled=True)
    down_in = pick_columns(hidden, down_tab[3], down_tab[2])
    out_terms = jnp.einsum("tsn,snk->tsk", down_in, down_w, preferred_element_type=jnp.float32)
    out_part = into_rows(out_terms, down_tab[1]).reshape(tok_count, -1)
    layer_out = lax.psum_scatter(
        out_part.astype(jnp.bfloat16), "tensor", scatter_dimension=1, tiled=True
    )
    full_grads = lax.all_gather(cotangent, "tensor", axis=1, tiled=True)
    grad_blocks = full_grads.reshape(tok_count, feature_count, side)
    down_back = jnp.take(grad_blocks, slot_rows[2], axis=1)
    down_part = jnp.einsum("tsn,tsk->snk", down_in, down_back, preferred_element_type=jnp.float32)
    back_terms = jnp.einsum("tsk,snk->tsn", down_back, down_w, preferred_element_type=jnp.float32)
    dhidden = into_columns(back_terms, down_tab[0])
    dgate = (dhidden * up_pre * sigma_gate * (1.0 + gate_pre * (1.0 - sigma_gate))).astype(
        jnp.bfloat16
    )
    dup = (dhidden * active).astype(jnp.bfloat16)
    gate_back = pick_columns(dgate, gate_tab[3], gate_tab[2])
    up_back = pick_columns(dup, up_tab[3], up_tab[2])
    gate_terms = jnp.einsum("tsn,skn->tsk", gate_back, gate_w, preferred_element_type=jnp.float32)
    up_terms = jnp.einsum("tsn,skn->tsk", up_back, up_w, preferred_element_type=jnp.float32)
    in_part = (into_rows(gate_terms, gate_tab[1]) + into_rows(up_terms, up_tab[1])).reshape(
        tok_count, -1
    )
    input_grad = lax.psum_scatter(
        in_part.astype(jnp.bfloat16), "tensor", scatter_dimension=1, tiled=True
    )
    gate_part = jnp.einsum("tsk,tsn->skn", gate_in, gate_back, preferred_element_type=jnp.float32)
    up_part = jnp.einsum("tsk,tsn->skn", up_in, up_back, preferred_element_type=jnp.float32)
    gate_sum, up_sum, down_sum = (
        lax.psum_scatter(
            gate_part.astype(jnp.bfloat16), "fsdp", scatter_dimension=0, tiled=True
        ).astype(jnp.float32),
        lax.psum_scatter(
            up_part.astype(jnp.bfloat16), "fsdp", scatter_dimension=0, tiled=True
        ).astype(jnp.float32),
        lax.psum_scatter(
            down_part.astype(jnp.bfloat16), "fsdp", scatter_dimension=0, tiled=True
        ).astype(jnp.float32),
    )
    gate_grad = gate_sum.astype(jnp.bfloat16)[None]
    up_grad = up_sum.astype(jnp.bfloat16)[None]
    down_grad = down_sum.astype(jnp.bfloat16)[None]
    return (layer_out, input_grad, gate_grad, up_grad, down_grad)


def block_pass(slots, width, shares, meta_ref, acts_ref, w_ref, y_ref, g_ref, gate, up, dhid, hid, dgate, dup, acc):
    n_tensor, tok, feats = acts_ref.shape[1:]
    side = w_ref.shape[-1]
    per_chunk = feats // side
    per_share = slots // shares
    trash, zero = width, width + 1

    def row_of(t, m, s):
        return meta_ref[t * 6 * slots + m * 2 * slots + s]

    def col_of(t, m, s, dead):
        col = meta_ref[t * 6 * slots + m * 2 * slots + slots + s]
        return jnp.where(col < width, col, dead)

    def act(which, row):
        lanes = pl.ds(pl.multiple_of(lax.rem(row, per_chunk) * side, side), side)
        return acts_ref[which, lax.div(row, per_chunk), :, lanes]

    def place(t, m, s):
        share, k = divmod(s, per_share)
        return share * n_tensor + t, pl.ds((m * per_share + k) * side, side)

    def weight(t, m, s):
        unit, rows = place(t, m, s)
        return w_ref[unit, rows, :]

    def dot(a, b, dims):
        return lax.dot_general(a, b, (dims, ((), ())), preferred_element_type=jnp.float32)

    plain, right_t, left_t = ((1,), (0,)), ((1,), (1,)), ((0,), (0,))
    acc[...] = jnp.zeros_like(acc)

    @pl.loop(0, n_tensor)
    def _(t):
        gate[...] = jnp.zeros_like(gate)
        up[...] = jnp.zeros_like(up)
        dhid[...] = jnp.zeros_like(dhid)
        for m, which, dims, into in ((0, 0, plain, gate), (1, 0, plain, up), (2, 1, right_t, dhid)):
            terms = [dot(act(which, row_of(t, m, s)), weight(t, m, s), dims) for s in range(slots)]
            for s in range(slots):
                into[col_of(t, m, s, trash)] += terms[s]

        @pl.loop(0, width)
        def _(c):
            g, u, d = gate[c], up[c], dhid[c]
            sig = jax.nn.sigmoid(g)
            active = g * sig
            hid[c] = (active * u).astype(hid.dtype)
            dgate[c] = (d * u * sig * (1.0 + g * (1.0 - sig))).astype(dgate.dtype)
            dup[c] = (d * active).astype(dup.dtype)

        for ref in (hid, dgate, dup):
            ref[zero] = jnp.zeros_like(ref[zero])

        for m, which, vals, dims, out in ((2, 1, hid, plain, 0), (0, 0, dgate, right_t, 1), (1, 0, dup, right_t, 1)):
            rows = [row_of(t, m, s) for s in range(slots)]
            picked = [vals[col_of(t, m, s, zero)] for s in range(slots)]
            terms = [dot(picked[s], weight(t, m, s), dims) for s in range(slots)]
            for s in range(slots):
                unit, at = place(t, m, s)
                other = act(which, rows[s])
                pair = (picked[s], other) if m == 2 else (other, picked[s])
                g_ref[unit, at, :] = dot(*pair, left_t).astype(g_ref.dtype)
            for s in range(slots):
                acc[out, rows[s]] += terms[s]

    for out in range(2):
        for chunk in range(n_tensor):
            for j in range(per_chunk):
                y_ref[out, chunk, :, pl.ds(j * side, side)] = acc[out, chunk * per_chunk + j].astype(y_ref.dtype)


def run_blocks(meta, acts, weights, slots, width, shares):
    n_tensor, tok, feats = acts.shape[1:]
    units, _, side = weights.shape
    vmem = pl.BlockSpec(memory_space=pltpu.VMEM)
    cols = (width + 2, tok, side)
    return pl.pallas_call(
        functools.partial(block_pass, slots, width, shares),
        out_shape=(
            jax.ShapeDtypeStruct(acts.shape, acts.dtype),
            jax.ShapeDtypeStruct((units, 3 * slots // shares * side, side), weights.dtype),
        ),
        in_specs=[pl.BlockSpec(memory_space=pltpu.SMEM), vmem, vmem],
        out_specs=(vmem, vmem),
        scratch_shapes=[pltpu.VMEM(cols, jnp.float32)] * 3
        + [pltpu.VMEM(cols, jnp.bfloat16)] * 3
        + [pltpu.VMEM((2, n_tensor * feats // side, tok, side), jnp.float32)],
        compiler_params=pltpu.CompilerParams(vmem_limit_bytes=48 * 1024 * 1024),
    )(meta, acts, weights)


def pack_unit(gate_blocks, up_blocks, down_blocks, block_rows, col_counts):
    slots = block_rows.shape[-1]
    side = gate_blocks.shape[-1]
    cols = jax.vmap(lambda c: slot_columns(c, slots))(col_counts[:, 0, :])
    table = jnp.concatenate([block_rows[:, 0, :], cols], axis=1).reshape(-1)
    table = jnp.pad(table, (0, 16 * side - table.shape[0])).reshape(16, side)
    blocks = [b[0].reshape(-1, side) for b in (gate_blocks, up_blocks, down_blocks)]
    return jnp.concatenate(blocks + [table.astype(jnp.bfloat16)], axis=0)


def spread_plan(n_fsdp, n_tensor, tokens, cotangent, gate_blocks, up_blocks, down_blocks, block_rows, col_counts):
    slots, width = block_rows.shape[-1], col_counts.shape[-1]
    tok_count, feats = tokens.shape
    side = gate_blocks.shape[-1]
    per_share = slots // n_fsdp
    unit = pack_unit(gate_blocks, up_blocks, down_blocks, block_rows, col_counts)
    acts = jnp.stack([tokens, cotangent]).reshape(2, n_tensor, tok_count // n_tensor, feats)
    weights, acts = bring(n_fsdp, n_tensor, unit, acts)
    meta = weights[:n_tensor, -16:, :].astype(jnp.int32).reshape(n_tensor, -1)
    meta = meta[:, : 6 * slots].reshape(-1)
    y, grads = run_blocks(meta, acts, weights, slots, width, n_fsdp)
    y, own = send_back(n_fsdp, n_tensor, y, grads)
    y = y.reshape(2, tok_count, feats)
    own = own.reshape(3, 1, per_share, side, side)
    return y[0], y[1], own[0], own[1], own[2]


def bring(n_fsdp, n_tensor, unit, acts):
    weights = lax.all_gather(unit, ("fsdp", "tensor"), axis=0)
    return weights, lax.all_to_all(acts, "tensor", 1, 1, tiled=True)


def send_back(n_fsdp, n_tensor, y, grads):
    own = lax.psum_scatter(grads, ("fsdp", "tensor"), scatter_dimension=0, tiled=True)
    return lax.all_to_all(y, "tensor", 1, 1, tiled=True), own[0]


def solution(mesh):
    n_fsdp, n_tensor = mesh.shape["fsdp"], mesh.shape["tensor"]

    def on_device(*args):
        block_bytes = 3 * args[2].size * args[2].dtype.itemsize * n_fsdp * n_tensor
        if block_bytes <= 8 * 1024 * 1024 and args[0].shape[0] % (16 * n_tensor) == 0:
            return spread_plan(n_fsdp, n_tensor, *args)
        return gathered_plan(*args)

    in_specs = (
        P(("group", "fsdp"), "tensor"),
        P(("group", "fsdp"), "tensor"),
        P("tensor", "fsdp", None, None),
        P("tensor", "fsdp", None, None),
        P("tensor", "fsdp", None, None),
        P(None, "tensor", None),
        P(None, "tensor", None),
    )
    out_specs = (
        P(("group", "fsdp"), "tensor"),
        P(("group", "fsdp"), "tensor"),
        P(("group", "tensor"), "fsdp", None, None),
        P(("group", "tensor"), "fsdp", None, None),
        P(("group", "tensor"), "fsdp", None, None),
    )
    return jax.shard_map(
        on_device, mesh=mesh, in_specs=in_specs, out_specs=out_specs, check_vma=False
    )
```

```python
import functools

import jax
import jax.numpy as jnp
from jax import lax
from jax.experimental import pallas as pl
from jax.experimental.pallas import tpu as pltpu
from jax.sharding import PartitionSpec as P

finest = lax.Precision.HIGHEST


def slot_columns(counts, slot_count):
    running = jnp.cumsum(counts)
    places = lax.broadcasted_iota(jnp.int32, (slot_count, counts.shape[0]), 0)
    return jnp.sum((running[None, :] <= places).astype(jnp.int32), axis=1)


def slot_tables(slot_rows, counts, feature_count):
    slot_count = slot_rows.shape[0]
    col_width = counts.shape[0]
    columns = slot_columns(counts, slot_count)
    col_hot = (
        columns[:, None] == lax.broadcasted_iota(jnp.int32, (slot_count, col_width), 1)
    ).astype(jnp.float32)
    row_hot = (
        slot_rows[:, None] == lax.broadcasted_iota(jnp.int32, (slot_count, feature_count), 1)
    ).astype(jnp.float32)
    is_live = columns < col_width
    picker = jnp.minimum(columns, col_width - 1)
    return (col_hot, row_hot, is_live, picker)


def into_columns(terms, col_hot):
    return jnp.einsum("tsn,sc->tcn", terms, col_hot, precision=finest)


def into_rows(terms, row_hot):
    return jnp.einsum("tsk,sr->trk", terms, row_hot, precision=finest)


def pick_columns(values, picker, is_live):
    chosen = jnp.take(values, picker, axis=1)
    return jnp.where(is_live[None, :, None], chosen, jnp.zeros_like(chosen))


def gathered_plan(tokens, cotangent, gate_blocks, up_blocks, down_blocks, block_rows, col_counts):
    full_tokens = lax.all_gather(tokens, "tensor", axis=1, tiled=True)
    gate_w, up_w = (
        lax.all_gather(gate_blocks[0], "fsdp", axis=0, tiled=True),
        lax.all_gather(up_blocks[0], "fsdp", axis=0, tiled=True),
    )
    slot_rows = block_rows[:, 0, :]
    counts = col_counts[:, 0, :]
    tok_count = full_tokens.shape[0]
    side = gate_w.shape[-1]
    feature_count = full_tokens.shape[1] // side
    token_blocks = full_tokens.reshape(tok_count, feature_count, side)
    gate_tab = slot_tables(slot_rows[0], counts[0], feature_count)
    up_tab = slot_tables(slot_rows[1], counts[1], feature_count)
    down_tab = slot_tables(slot_rows[2], counts[2], feature_count)
    gate_in = jnp.take(token_blocks, slot_rows[0], axis=1)
    up_in = jnp.take(token_blocks, slot_rows[1], axis=1)
    gate_pre = into_columns(
        jnp.einsum("tsk,skn->tsn", gate_in, gate_w, preferred_element_type=jnp.float32), gate_tab[0]
    )
    up_pre = into_columns(
        jnp.einsum("tsk,skn->tsn", up_in, up_w, preferred_element_type=jnp.float32), up_tab[0]
    )
    sigma_gate = jax.nn.sigmoid(gate_pre)
    active = gate_pre * sigma_gate
    hidden = (active * up_pre).astype(jnp.bfloat16)
    down_w = lax.all_gather(down_blocks[0], "fsdp", axis=0, tiled=True)
    down_in = pick_columns(hidden, down_tab[3], down_tab[2])
    out_terms = jnp.einsum("tsn,snk->tsk", down_in, down_w, preferred_element_type=jnp.float32)
    out_part = into_rows(out_terms, down_tab[1]).reshape(tok_count, -1)
    layer_out = lax.psum_scatter(
        out_part.astype(jnp.bfloat16), "tensor", scatter_dimension=1, tiled=True
    )
    full_grads = lax.all_gather(cotangent, "tensor", axis=1, tiled=True)
    grad_blocks = full_grads.reshape(tok_count, feature_count, side)
    down_back = jnp.take(grad_blocks, slot_rows[2], axis=1)
    down_part = jnp.einsum("tsn,tsk->snk", down_in, down_back, preferred_element_type=jnp.float32)
    back_terms = jnp.einsum("tsk,snk->tsn", down_back, down_w, preferred_element_type=jnp.float32)
    dhidden = into_columns(back_terms, down_tab[0])
    dgate = (dhidden * up_pre * sigma_gate * (1.0 + gate_pre * (1.0 - sigma_gate))).astype(
        jnp.bfloat16
    )
    dup = (dhidden * active).astype(jnp.bfloat16)
    gate_back = pick_columns(dgate, gate_tab[3], gate_tab[2])
    up_back = pick_columns(dup, up_tab[3], up_tab[2])
    gate_terms = jnp.einsum("tsn,skn->tsk", gate_back, gate_w, preferred_element_type=jnp.float32)
    up_terms = jnp.einsum("tsn,skn->tsk", up_back, up_w, preferred_element_type=jnp.float32)
    in_part = (into_rows(gate_terms, gate_tab[1]) + into_rows(up_terms, up_tab[1])).reshape(
        tok_count, -1
    )
    input_grad = lax.psum_scatter(
        in_part.astype(jnp.bfloat16), "tensor", scatter_dimension=1, tiled=True
    )
    gate_part = jnp.einsum("tsk,tsn->skn", gate_in, gate_back, preferred_element_type=jnp.float32)
    up_part = jnp.einsum("tsk,tsn->skn", up_in, up_back, preferred_element_type=jnp.float32)
    gate_sum, up_sum, down_sum = (
        lax.psum_scatter(
            gate_part.astype(jnp.bfloat16), "fsdp", scatter_dimension=0, tiled=True
        ).astype(jnp.float32),
        lax.psum_scatter(
            up_part.astype(jnp.bfloat16), "fsdp", scatter_dimension=0, tiled=True
        ).astype(jnp.float32),
        lax.psum_scatter(
            down_part.astype(jnp.bfloat16), "fsdp", scatter_dimension=0, tiled=True
        ).astype(jnp.float32),
    )
    gate_grad = gate_sum.astype(jnp.bfloat16)[None]
    up_grad = up_sum.astype(jnp.bfloat16)[None]
    down_grad = down_sum.astype(jnp.bfloat16)[None]
    return (layer_out, input_grad, gate_grad, up_grad, down_grad)


def block_pass(slots, width, shares, meta_ref, acts_ref, w_ref, y_ref, g_ref, gate, up, dhid, hid, dgate, dup, acc):
    n_tensor, tok, feats = acts_ref.shape[1:]
    side = w_ref.shape[-1]
    per_chunk = feats // side
    per_share = slots // shares
    trash, zero = width, width + 1

    def row_of(t, m, s):
        return meta_ref[t * 6 * slots + m * 2 * slots + s]

    def col_of(t, m, s, dead):
        col = meta_ref[t * 6 * slots + m * 2 * slots + slots + s]
        return jnp.where(col < width, col, dead)

    def act(which, row):
        lanes = pl.ds(pl.multiple_of(lax.rem(row, per_chunk) * side, side), side)
        return acts_ref[which, lax.div(row, per_chunk), :, lanes]

    def place(t, m, s):
        share, k = divmod(s, per_share)
        return share * n_tensor + t, pl.ds((m * per_share + k) * side, side)

    def weight(t, m, s):
        unit, rows = place(t, m, s)
        return w_ref[unit, rows, :]

    def dot(a, b, dims):
        return lax.dot_general(a, b, (dims, ((), ())), preferred_element_type=jnp.float32)

    plain, right_t, left_t = ((1,), (0,)), ((1,), (1,)), ((0,), (0,))
    acc[...] = jnp.zeros_like(acc)

    @pl.loop(0, n_tensor)
    def _(t):
        gate[...] = jnp.zeros_like(gate)
        up[...] = jnp.zeros_like(up)
        dhid[...] = jnp.zeros_like(dhid)
        for m, which, dims, into in ((0, 0, plain, gate), (1, 0, plain, up), (2, 1, right_t, dhid)):
            terms = [dot(act(which, row_of(t, m, s)), weight(t, m, s), dims) for s in range(slots)]
            for s in range(slots):
                into[col_of(t, m, s, trash)] += terms[s]

        @pl.loop(0, width)
        def _(c):
            g, u, d = gate[c], up[c], dhid[c]
            sig = jax.nn.sigmoid(g)
            active = g * sig
            hid[c] = (active * u).astype(hid.dtype)
            dgate[c] = (d * u * sig * (1.0 + g * (1.0 - sig))).astype(dgate.dtype)
            dup[c] = (d * active).astype(dup.dtype)

        for ref in (hid, dgate, dup):
            ref[zero] = jnp.zeros_like(ref[zero])

        for m, which, vals, dims, out in ((2, 1, hid, plain, 0), (0, 0, dgate, right_t, 1), (1, 0, dup, right_t, 1)):
            rows = [row_of(t, m, s) for s in range(slots)]
            picked = [vals[col_of(t, m, s, zero)] for s in range(slots)]
            terms = [dot(picked[s], weight(t, m, s), dims) for s in range(slots)]
            for s in range(slots):
                unit, at = place(t, m, s)
                other = act(which, rows[s])
                pair = (picked[s], other) if m == 2 else (other, picked[s])
                g_ref[unit, at, :] = dot(*pair, left_t).astype(g_ref.dtype)
            for s in range(slots):
                acc[out, rows[s]] += terms[s]

    for out in range(2):
        for chunk in range(n_tensor):
            for j in range(per_chunk):
                y_ref[out, chunk, :, pl.ds(j * side, side)] = acc[out, chunk * per_chunk + j].astype(y_ref.dtype)


def run_blocks(meta, acts, weights, slots, width, shares):
    n_tensor, tok, feats = acts.shape[1:]
    units, _, side = weights.shape
    vmem = pl.BlockSpec(memory_space=pltpu.VMEM)
    cols = (width + 2, tok, side)
    return pl.pallas_call(
        functools.partial(block_pass, slots, width, shares),
        out_shape=(
            jax.ShapeDtypeStruct(acts.shape, acts.dtype),
            jax.ShapeDtypeStruct((units, 3 * slots // shares * side, side), weights.dtype),
        ),
        in_specs=[pl.BlockSpec(memory_space=pltpu.SMEM), vmem, vmem],
        out_specs=(vmem, vmem),
        scratch_shapes=[pltpu.VMEM(cols, jnp.float32)] * 3
        + [pltpu.VMEM(cols, jnp.bfloat16)] * 3
        + [pltpu.VMEM((2, n_tensor * feats // side, tok, side), jnp.float32)],
        compiler_params=pltpu.CompilerParams(vmem_limit_bytes=48 * 1024 * 1024),
    )(meta, acts, weights)


def pack_unit(gate_blocks, up_blocks, down_blocks, block_rows, col_counts):
    slots = block_rows.shape[-1]
    side = gate_blocks.shape[-1]
    cols = jax.vmap(lambda c: slot_columns(c, slots))(col_counts[:, 0, :])
    table = jnp.concatenate([block_rows[:, 0, :], cols], axis=1).reshape(-1)
    table = jnp.pad(table, (0, 32 * side - table.shape[0])).reshape(32, side)
    blocks = [b[0].reshape(-1, side) for b in (gate_blocks, up_blocks, down_blocks)]
    return jnp.concatenate(blocks + [table.astype(jnp.bfloat16)], axis=0)


def spread_plan(n_fsdp, n_tensor, tokens, cotangent, gate_blocks, up_blocks, down_blocks, block_rows, col_counts):
    slots, width = block_rows.shape[-1], col_counts.shape[-1]
    unit = pack_unit(gate_blocks, up_blocks, down_blocks, block_rows, col_counts)
    weights, acts = bring(n_fsdp, n_tensor, unit, tokens, cotangent)
    meta = weights[:n_tensor, -32:, :].astype(jnp.int32).reshape(n_tensor, -1)
    meta = meta[:, : 6 * slots].reshape(-1)
    y, grads = run_blocks(meta, acts, weights, slots, width, n_fsdp)
    return send_back(n_fsdp, n_tensor, y, grads)


def greet(peers):
    barrier = pltpu.get_barrier_semaphore()
    for peer in peers:
        pl.semaphore_signal(barrier, inc=1, device_id=peer, device_id_type=pl.DeviceIdType.MESH)
    pl.semaphore_wait(barrier, len(peers))


def remote(src, dst, send_sem, recv_sem, peer):
    return pltpu.make_async_remote_copy(
        src_ref=src, dst_ref=dst, send_sem=send_sem, recv_sem=recv_sem,
        device_id=peer, device_id_type=pl.DeviceIdType.MESH,
    )


def bring_kernel(
    n_tensor, unit_ref, tok_ref, cot_ref, w_ref, acts_ref,
    z_send, y_send, x_send, c_send, a_send, z_recv, y_recv, x_recv, c_recv, a_recv, own_sem,
):
    group, f, t = (lax.axis_index(a) for a in ("group", "fsdp", "tensor"))
    f_core = f + 1 - 2 * lax.rem(f, 2)
    f_y = lax.rem(f + 2, 4)
    f_diag = f_core + f_y - f
    x_peer, y_peer, c_peer = {"group": 1 - group}, {"fsdp": f_y}, {"fsdp": f_core}
    others = [lax.rem(t + d, n_tensor) for d in range(1, n_tensor)]
    greet([{"tensor": o} for o in others] + [x_peer, y_peer, c_peer])

    half = unit_ref.shape[0] // 2
    mine = pl.ds(pl.multiple_of(group * half, 16), half)
    theirs = pl.ds(pl.multiple_of((1 - group) * half, 16), half)
    rows = tok_ref.shape[0] // n_tensor

    def at(ff, tt):
        return ff * n_tensor + tt

    def chunk(tt):
        return pl.ds(pl.multiple_of(tt * rows, 16), rows)

    sends = []

    def go(copy):
        copy.start()
        sends.append(copy)

    def arrived(view, sem):
        remote(view, view, own_sem.at[0], sem, c_peer).wait_recv()

    me = at(f, t)
    for d, o in enumerate(others):
        go(remote(unit_ref.at[mine], w_ref.at[me, mine], z_send.at[d], z_recv.at[t], {"tensor": o}))
    go(remote(unit_ref.at[mine], w_ref.at[me, mine], y_send.at[n_tensor - 1], y_recv.at[t], y_peer))
    go(remote(unit_ref, w_ref.at[me], c_send.at[0], c_recv.at[at(0, t)], c_peer))
    locals_ = [pltpu.make_async_copy(unit_ref, w_ref.at[me], own_sem.at[1])]
    for i, ref in enumerate((tok_ref, cot_ref)):
        locals_.append(pltpu.make_async_copy(ref.at[chunk(t)], acts_ref.at[i, t], own_sem.at[2 + i]))
    for copy in locals_:
        copy.start()

    arrived(w_ref.at[at(f_y, t), mine], y_recv.at[t])
    part = w_ref.at[at(f_y, t), mine]
    go(remote(part, part, x_send.at[0], x_recv.at[at(1, t)], x_peer))
    for d, o in enumerate(others):
        part = w_ref.at[at(f, o), mine]
        arrived(part, z_recv.at[o])
        go(remote(part, part, y_send.at[d], y_recv.at[o], y_peer))
        go(remote(part, part, x_send.at[1 + d], x_recv.at[at(0, o)], x_peer))
    for d, o in enumerate(others):
        for i, ref in enumerate((tok_ref, cot_ref)):
            go(remote(ref.at[chunk(o)], acts_ref.at[i, t], a_send.at[2 * d + i], a_recv.at[2 * t + i], {"tensor": o}))
    for d, o in enumerate(others):
        part = w_ref.at[at(f_y, o), mine]
        arrived(part, y_recv.at[o])
        go(remote(part, part, x_send.at[n_tensor + d], x_recv.at[at(1, o)], x_peer))
    part = w_ref.at[at(f_y, t)]
    arrived(w_ref.at[at(f_y, t), theirs], x_recv.at[at(1, t)])
    go(remote(part, part, c_send.at[1], c_recv.at[at(1, t)], c_peer))
    for k, ff in enumerate((f, f_y)):
        for d, o in enumerate(others):
            part = w_ref.at[at(ff, o)]
            arrived(w_ref.at[at(ff, o), theirs], x_recv.at[at(k, o)])
            go(remote(part, part, c_send.at[2 + k * (n_tensor - 1) + d], c_recv.at[at(k, o)], c_peer))
    for k, ff in enumerate((f_core, f_diag)):
        for o in [t] + others:
            arrived(w_ref.at[at(ff, o)], c_recv.at[at(k, o)])
    for o in others:
        for i in range(2):
            arrived(acts_ref.at[i, o], a_recv.at[2 * o + i])
    for copy in locals_:
        copy.wait()
    for copy in sends:
        copy.wait_send()


def bring(n_fsdp, n_tensor, unit, tokens, cotangent):
    tok_count, feats = tokens.shape
    anywhere = pl.BlockSpec(memory_space=pl.ANY)
    sem = pltpu.SemaphoreType.DMA
    return pl.pallas_call(
        functools.partial(bring_kernel, n_tensor),
        out_shape=(
            jax.ShapeDtypeStruct((n_fsdp * n_tensor,) + unit.shape, unit.dtype),
            jax.ShapeDtypeStruct((2, n_tensor, tok_count // n_tensor, feats), tokens.dtype),
        ),
        in_specs=[anywhere] * 3,
        out_specs=(anywhere,) * 2,
        scratch_shapes=[
            sem((n_tensor - 1,)), sem((n_tensor,)), sem((2 * n_tensor - 1,)), sem((2 * n_tensor,)), sem((2 * n_tensor - 2,)),
            sem((n_tensor,)), sem((n_tensor,)), sem((2 * n_tensor,)), sem((2 * n_tensor,)), sem((2 * n_tensor,)), sem((4,)),
        ],
        compiler_params=pltpu.CompilerParams(collective_id=0, has_side_effects=True),
    )(unit, tokens, cotangent)


def return_kernel(
    n_tensor, y_ref, g_ref, out_ref, back_ref, gate_ref, up_ref, down_ref,
    c_buf, y_out, y_buf, z_out, z_buf, c_send, y_send, z_send, a_send, c_recv, y_recv, z_recv, a_recv, own_sem,
):
    f, t = lax.axis_index("fsdp"), lax.axis_index("tensor")
    f_core = f + 1 - 2 * lax.rem(f, 2)
    f_y = lax.rem(f + 2, 4)
    f_diag = f_core + f_y - f
    y_peer, c_peer = {"fsdp": f_y}, {"fsdp": f_core}
    others = [lax.rem(t + d, n_tensor) for d in range(1, n_tensor)]
    greet([{"tensor": o} for o in others] + [y_peer, c_peer])

    rows = y_ref.shape[2]
    side = g_ref.shape[-1]
    pieces = g_ref.shape[1] // side
    mine = pl.ds(pl.multiple_of(t * rows, 16), rows)
    order = others + [t]
    outs = (out_ref, back_ref)
    sends = []

    def at(ff, tt):
        return ff * n_tensor + tt

    def go(copy):
        copy.start()
        sends.append(copy)

    def arrived(view, sem):
        remote(view, view, own_sem.at[2], sem, c_peer).wait_recv()

    for k, ff in ((1, f_diag), (0, f_core)):
        for d, o in enumerate(order):
            go(remote(g_ref.at[at(ff, o)], c_buf.at[at(k, o)], c_send.at[at(k, d)], c_recv.at[at(k, o)], c_peer))
    for d, o in enumerate(others):
        for i in range(2):
            go(remote(y_ref.at[i, o], outs[i].at[mine], a_send.at[2 * d + i], a_recv.at[2 * t + i], {"tensor": o}))
    locals_ = [pltpu.make_async_copy(y_ref.at[i, t], outs[i].at[mine], own_sem.at[i]) for i in range(2)]
    for copy in locals_:
        copy.start()

    def total(j, *parts):
        spot = pl.ds(pl.multiple_of(j * side, side), side)
        return sum(p[i, spot, :].astype(jnp.float32) for p, i in parts)

    for d, o in enumerate(order):
        arrived(c_buf.at[at(1, o)], c_recv.at[at(1, o)])

        @pl.loop(0, pieces)
        def _(j):
            spot = pl.ds(pl.multiple_of(j * side, side), side)
            y_out[d, spot, :] = total(j, (g_ref, at(f_y, o)), (c_buf, at(1, o))).astype(y_out.dtype)

        go(remote(y_out.at[d], y_buf.at[o], y_send.at[d], y_recv.at[o], y_peer))
    for d, o in enumerate(others):
        arrived(c_buf.at[at(0, o)], c_recv.at[at(0, o)])
        arrived(y_buf.at[o], y_recv.at[o])

        @pl.loop(0, pieces)
        def _(j):
            spot = pl.ds(pl.multiple_of(j * side, side), side)
            parts = (g_ref, at(f, o)), (c_buf, at(0, o)), (y_buf, o)
            z_out[d, spot, :] = total(j, *parts).astype(z_out.dtype)

        go(remote(z_out.at[d], z_buf.at[t], z_send.at[d], z_recv.at[t], {"tensor": o}))
    arrived(c_buf.at[at(0, t)], c_recv.at[at(0, t)])
    arrived(y_buf.at[t], y_recv.at[t])
    for o in others:
        arrived(z_buf.at[o], z_recv.at[o])
    per_share = pieces // 3
    for m, ref in enumerate((gate_ref, up_ref, down_ref)):
        for k in range(per_share):
            parts = [(g_ref, at(f, t)), (c_buf, at(0, t)), (y_buf, t)] + [(z_buf, o) for o in others]
            ref[0, k] = total(m * per_share + k, *parts).astype(ref.dtype)
    for o in others:
        for i in range(2):
            spot = pl.ds(pl.multiple_of(o * rows, 16), rows)
            arrived(outs[i].at[spot], a_recv.at[2 * o + i])
    for copy in locals_:
        copy.wait()
    for copy in sends:
        copy.wait_send()


def send_back(n_fsdp, n_tensor, y, grads):
    rows, feats = y.shape[2:]
    side = grads.shape[-1]
    unit = grads.shape[1:]
    per_share = unit[0] // (3 * side)
    anywhere, vmem = pl.BlockSpec(memory_space=pl.ANY), pl.BlockSpec(memory_space=pltpu.VMEM)
    sem = pltpu.SemaphoreType.DMA
    big = jax.ShapeDtypeStruct((n_tensor * rows, feats), y.dtype)
    small = jax.ShapeDtypeStruct((1, per_share, side, side), grads.dtype)

    def buf(count):
        return pltpu.VMEM((count,) + unit, grads.dtype)

    return pl.pallas_call(
        functools.partial(return_kernel, n_tensor),
        out_shape=(big, big, small, small, small),
        in_specs=[anywhere, vmem],
        out_specs=(anywhere, anywhere, vmem, vmem, vmem),
        scratch_shapes=[
            buf(2 * n_tensor), buf(n_tensor), buf(n_tensor), buf(n_tensor - 1), buf(n_tensor),
            sem((2 * n_tensor,)), sem((n_tensor,)), sem((n_tensor - 1,)), sem((2 * n_tensor - 2,)),
            sem((2 * n_tensor,)), sem((n_tensor,)), sem((n_tensor,)), sem((2 * n_tensor,)), sem((3,)),
        ],
        compiler_params=pltpu.CompilerParams(
            collective_id=1, has_side_effects=True, vmem_limit_bytes=40 * 1024 * 1024
        ),
    )(y, grads)


def solution(mesh):
    n_fsdp, n_tensor = mesh.shape["fsdp"], mesh.shape["tensor"]

    def on_device(*args):
        block_bytes = 3 * args[2].size * args[2].dtype.itemsize * n_fsdp * n_tensor
        known = mesh.shape["group"] == 2 and n_fsdp == 4
        if known and block_bytes <= 8 * 1024 * 1024 and args[0].shape[0] % (16 * n_tensor) == 0:
            return spread_plan(n_fsdp, n_tensor, *args)
        return gathered_plan(*args)

    in_specs = (
        P(("group", "fsdp"), "tensor"),
        P(("group", "fsdp"), "tensor"),
        P("tensor", "fsdp", None, None),
        P("tensor", "fsdp", None, None),
        P("tensor", "fsdp", None, None),
        P(None, "tensor", None),
        P(None, "tensor", None),
    )
    out_specs = (
        P(("group", "fsdp"), "tensor"),
        P(("group", "fsdp"), "tensor"),
        P(("group", "tensor"), "fsdp", None, None),
        P(("group", "tensor"), "fsdp", None, None),
        P(("group", "tensor"), "fsdp", None, None),
    )
    return jax.shard_map(
        on_device, mesh=mesh, in_specs=in_specs, out_specs=out_specs, check_vma=False
    )
```

```python
import functools

import jax
import jax.numpy as jnp
from jax import lax
from jax.experimental import pallas as pl
from jax.experimental.pallas import tpu as pltpu
from jax.sharding import PartitionSpec as P

finest = lax.Precision.HIGHEST


def slot_columns(counts, slot_count):
    running = jnp.cumsum(counts)
    places = lax.broadcasted_iota(jnp.int32, (slot_count, counts.shape[0]), 0)
    return jnp.sum((running[None, :] <= places).astype(jnp.int32), axis=1)


def slot_tables(slot_rows, counts, feature_count):
    slot_count = slot_rows.shape[0]
    col_width = counts.shape[0]
    columns = slot_columns(counts, slot_count)
    col_hot = (
        columns[:, None] == lax.broadcasted_iota(jnp.int32, (slot_count, col_width), 1)
    ).astype(jnp.float32)
    row_hot = (
        slot_rows[:, None] == lax.broadcasted_iota(jnp.int32, (slot_count, feature_count), 1)
    ).astype(jnp.float32)
    is_live = columns < col_width
    picker = jnp.minimum(columns, col_width - 1)
    return (col_hot, row_hot, is_live, picker)


def into_columns(terms, col_hot):
    return jnp.einsum("tsn,sc->tcn", terms, col_hot, precision=finest)


def into_rows(terms, row_hot):
    return jnp.einsum("tsk,sr->trk", terms, row_hot, precision=finest)


def pick_columns(values, picker, is_live):
    chosen = jnp.take(values, picker, axis=1)
    return jnp.where(is_live[None, :, None], chosen, jnp.zeros_like(chosen))


def gathered_plan(tokens, cotangent, gate_blocks, up_blocks, down_blocks, block_rows, col_counts):
    full_tokens = lax.all_gather(tokens, "tensor", axis=1, tiled=True)
    gate_w, up_w = (
        lax.all_gather(gate_blocks[0], "fsdp", axis=0, tiled=True),
        lax.all_gather(up_blocks[0], "fsdp", axis=0, tiled=True),
    )
    slot_rows = block_rows[:, 0, :]
    counts = col_counts[:, 0, :]
    tok_count = full_tokens.shape[0]
    side = gate_w.shape[-1]
    feature_count = full_tokens.shape[1] // side
    token_blocks = full_tokens.reshape(tok_count, feature_count, side)
    gate_tab = slot_tables(slot_rows[0], counts[0], feature_count)
    up_tab = slot_tables(slot_rows[1], counts[1], feature_count)
    down_tab = slot_tables(slot_rows[2], counts[2], feature_count)
    gate_in = jnp.take(token_blocks, slot_rows[0], axis=1)
    up_in = jnp.take(token_blocks, slot_rows[1], axis=1)
    gate_pre = into_columns(
        jnp.einsum("tsk,skn->tsn", gate_in, gate_w, preferred_element_type=jnp.float32), gate_tab[0]
    )
    up_pre = into_columns(
        jnp.einsum("tsk,skn->tsn", up_in, up_w, preferred_element_type=jnp.float32), up_tab[0]
    )
    sigma_gate = jax.nn.sigmoid(gate_pre)
    active = gate_pre * sigma_gate
    hidden = (active * up_pre).astype(jnp.bfloat16)
    down_w = lax.all_gather(down_blocks[0], "fsdp", axis=0, tiled=True)
    down_in = pick_columns(hidden, down_tab[3], down_tab[2])
    out_terms = jnp.einsum("tsn,snk->tsk", down_in, down_w, preferred_element_type=jnp.float32)
    out_part = into_rows(out_terms, down_tab[1]).reshape(tok_count, -1)
    layer_out = lax.psum_scatter(
        out_part.astype(jnp.bfloat16), "tensor", scatter_dimension=1, tiled=True
    )
    full_grads = lax.all_gather(cotangent, "tensor", axis=1, tiled=True)
    grad_blocks = full_grads.reshape(tok_count, feature_count, side)
    down_back = jnp.take(grad_blocks, slot_rows[2], axis=1)
    down_part = jnp.einsum("tsn,tsk->snk", down_in, down_back, preferred_element_type=jnp.float32)
    back_terms = jnp.einsum("tsk,snk->tsn", down_back, down_w, preferred_element_type=jnp.float32)
    dhidden = into_columns(back_terms, down_tab[0])
    dgate = (dhidden * up_pre * sigma_gate * (1.0 + gate_pre * (1.0 - sigma_gate))).astype(
        jnp.bfloat16
    )
    dup = (dhidden * active).astype(jnp.bfloat16)
    gate_back = pick_columns(dgate, gate_tab[3], gate_tab[2])
    up_back = pick_columns(dup, up_tab[3], up_tab[2])
    gate_terms = jnp.einsum("tsn,skn->tsk", gate_back, gate_w, preferred_element_type=jnp.float32)
    up_terms = jnp.einsum("tsn,skn->tsk", up_back, up_w, preferred_element_type=jnp.float32)
    in_part = (into_rows(gate_terms, gate_tab[1]) + into_rows(up_terms, up_tab[1])).reshape(
        tok_count, -1
    )
    input_grad = lax.psum_scatter(
        in_part.astype(jnp.bfloat16), "tensor", scatter_dimension=1, tiled=True
    )
    gate_part = jnp.einsum("tsk,tsn->skn", gate_in, gate_back, preferred_element_type=jnp.float32)
    up_part = jnp.einsum("tsk,tsn->skn", up_in, up_back, preferred_element_type=jnp.float32)
    gate_sum, up_sum, down_sum = (
        lax.psum_scatter(
            gate_part.astype(jnp.bfloat16), "fsdp", scatter_dimension=0, tiled=True
        ).astype(jnp.float32),
        lax.psum_scatter(
            up_part.astype(jnp.bfloat16), "fsdp", scatter_dimension=0, tiled=True
        ).astype(jnp.float32),
        lax.psum_scatter(
            down_part.astype(jnp.bfloat16), "fsdp", scatter_dimension=0, tiled=True
        ).astype(jnp.float32),
    )
    gate_grad = gate_sum.astype(jnp.bfloat16)[None]
    up_grad = up_sum.astype(jnp.bfloat16)[None]
    down_grad = down_sum.astype(jnp.bfloat16)[None]
    return (layer_out, input_grad, gate_grad, up_grad, down_grad)


def block_pass(slots, width, shares, meta_ref, acts_ref, w_ref, y_ref, left_ref, right_ref, gate, up, dhid, hid, dgate, dup, acc):
    n_tensor, tok, feats = acts_ref.shape[1:]
    side = w_ref.shape[-1]
    per_chunk = feats // side
    per_share = slots // shares
    trash, zero = width, width + 1

    def row_of(t, m, s):
        return meta_ref[t * 6 * slots + m * 2 * slots + s]

    def col_of(t, m, s, dead):
        col = meta_ref[t * 6 * slots + m * 2 * slots + slots + s]
        return jnp.where(col < width, col, dead)

    def act(which, row):
        lanes = pl.ds(pl.multiple_of(lax.rem(row, per_chunk) * side, side), side)
        return acts_ref[which, lax.div(row, per_chunk), :, lanes]

    def place(t, m, s):
        share, k = divmod(s, per_share)
        return share * n_tensor + t, pl.ds((m * per_share + k) * side, side)

    def weight(t, m, s):
        unit, rows = place(t, m, s)
        return w_ref[unit, rows, :]

    def dot(a, b, dims):
        return lax.dot_general(a, b, (dims, ((), ())), preferred_element_type=jnp.float32)

    plain, right_t = ((1,), (0,)), ((1,), (1,))
    acc[...] = jnp.zeros_like(acc)

    @pl.loop(0, n_tensor)
    def _(t):
        gate[...] = jnp.zeros_like(gate)
        up[...] = jnp.zeros_like(up)
        dhid[...] = jnp.zeros_like(dhid)
        for m, which, dims, into in ((0, 0, plain, gate), (1, 0, plain, up), (2, 1, right_t, dhid)):
            terms = [dot(act(which, row_of(t, m, s)), weight(t, m, s), dims) for s in range(slots)]
            for s in range(slots):
                into[col_of(t, m, s, trash)] += terms[s]

        @pl.loop(0, width)
        def _(c):
            g, u, d = gate[c], up[c], dhid[c]
            sig = jax.nn.sigmoid(g)
            active = g * sig
            hid[c] = (active * u).astype(hid.dtype)
            dgate[c] = (d * u * sig * (1.0 + g * (1.0 - sig))).astype(dgate.dtype)
            dup[c] = (d * active).astype(dup.dtype)

        for ref in (hid, dgate, dup):
            ref[zero] = jnp.zeros_like(ref[zero])

        for m, which, vals, dims, out in ((2, 1, hid, plain, 0), (0, 0, dgate, right_t, 1), (1, 0, dup, right_t, 1)):
            rows = [row_of(t, m, s) for s in range(slots)]
            picked = [vals[col_of(t, m, s, zero)] for s in range(slots)]
            terms = [dot(picked[s], weight(t, m, s), dims) for s in range(slots)]
            for s in range(slots):
                unit, at = s // per_share * n_tensor + t, m * per_share + s % per_share
                other = act(which, rows[s])
                pair = (picked[s], other) if m == 2 else (other, picked[s])
                left_ref[unit, at] = pair[0]
                right_ref[unit, at] = pair[1]
            for s in range(slots):
                acc[out, rows[s]] += terms[s]

    for out in range(2):
        for chunk in range(n_tensor):
            for j in range(per_chunk):
                y_ref[out, chunk, :, pl.ds(j * side, side)] = acc[out, chunk * per_chunk + j].astype(y_ref.dtype)


def run_blocks(meta, acts, weights, slots, width, shares):
    n_tensor, tok, feats = acts.shape[1:]
    units, _, side = weights.shape
    vmem = pl.BlockSpec(memory_space=pltpu.VMEM)
    picked = jax.ShapeDtypeStruct((units, 3 * slots // shares, tok, side), acts.dtype)
    cols = (width + 2, tok, side)
    return pl.pallas_call(
        functools.partial(block_pass, slots, width, shares),
        out_shape=(jax.ShapeDtypeStruct(acts.shape, acts.dtype), picked, picked),
        in_specs=[pl.BlockSpec(memory_space=pltpu.SMEM), vmem, vmem],
        out_specs=(vmem, vmem, vmem),
        scratch_shapes=[pltpu.VMEM(cols, jnp.float32)] * 3
        + [pltpu.VMEM(cols, jnp.bfloat16)] * 3
        + [pltpu.VMEM((2, n_tensor * feats // side, tok, side), jnp.float32)],
        compiler_params=pltpu.CompilerParams(vmem_limit_bytes=48 * 1024 * 1024),
    )(meta, acts, weights)


def pack_unit(gate_blocks, up_blocks, down_blocks, block_rows, col_counts):
    slots = block_rows.shape[-1]
    side = gate_blocks.shape[-1]
    cols = jax.vmap(lambda c: slot_columns(c, slots))(col_counts[:, 0, :])
    table = jnp.concatenate([block_rows[:, 0, :], cols], axis=1).reshape(-1)
    table = jnp.pad(table, (0, 32 * side - table.shape[0])).reshape(32, side)
    blocks = [b[0].reshape(-1, side) for b in (gate_blocks, up_blocks, down_blocks)]
    return jnp.concatenate(blocks + [table.astype(jnp.bfloat16)], axis=0)


def spread_plan(n_fsdp, n_tensor, tokens, cotangent, gate_blocks, up_blocks, down_blocks, block_rows, col_counts):
    slots, width = block_rows.shape[-1], col_counts.shape[-1]
    unit = pack_unit(gate_blocks, up_blocks, down_blocks, block_rows, col_counts)
    weights, acts = bring(n_fsdp, n_tensor, unit, tokens, cotangent)
    meta = weights[:n_tensor, -32:, :].astype(jnp.int32).reshape(n_tensor, -1)
    meta = meta[:, : 6 * slots].reshape(-1)
    y, lefts, rights = run_blocks(meta, acts, weights, slots, width, n_fsdp)
    return send_back(n_tensor, y, lefts, rights)


def greet(peers):
    barrier = pltpu.get_barrier_semaphore()
    for peer in peers:
        pl.semaphore_signal(barrier, inc=1, device_id=peer, device_id_type=pl.DeviceIdType.MESH)
    pl.semaphore_wait(barrier, len(peers))


def remote(src, dst, send_sem, recv_sem, peer):
    return pltpu.make_async_remote_copy(
        src_ref=src, dst_ref=dst, send_sem=send_sem, recv_sem=recv_sem,
        device_id=peer, device_id_type=pl.DeviceIdType.MESH,
    )


def bring_kernel(
    n_tensor, unit_ref, tok_ref, cot_ref, w_ref, acts_ref,
    z_send, y_send, x_send, c_send, a_send, z_recv, y_recv, x_recv, c_recv, a_recv, own_sem,
):
    group, f, t = (lax.axis_index(a) for a in ("group", "fsdp", "tensor"))
    f_core = f + 1 - 2 * lax.rem(f, 2)
    f_y = lax.rem(f + 2, 4)
    f_diag = f_core + f_y - f
    x_peer, y_peer, c_peer = {"group": 1 - group}, {"fsdp": f_y}, {"fsdp": f_core}
    pair = t + 1 - 2 * lax.rem(t, 2)
    far = n_tensor - 1 - t
    others = [pair, far, n_tensor - 1 - pair]
    greet([{"tensor": o} for o in others] + [x_peer, y_peer, c_peer])

    half = unit_ref.shape[0] // 2
    mine = pl.ds(pl.multiple_of(group * half, 16), half)
    theirs = pl.ds(pl.multiple_of((1 - group) * half, 16), half)
    rows = tok_ref.shape[0] // n_tensor

    def at(ff, tt):
        return ff * n_tensor + tt

    def chunk(tt):
        return pl.ds(pl.multiple_of(tt * rows, 16), rows)

    sends = []

    def go(copy):
        copy.start()
        sends.append(copy)

    def arrived(view, sem):
        remote(view, view, own_sem.at[0], sem, c_peer).wait_recv()

    def share_acts():
        for d, o in enumerate(others):
            for i, ref in enumerate((tok_ref, cot_ref)):
                go(remote(ref.at[chunk(o)], acts_ref.at[i, t], a_send.at[2 * d + i], a_recv.at[2 * t + i], {"tensor": o}))

    me = at(f, t)
    for d, o in enumerate((far, pair)):
        go(remote(unit_ref.at[mine], w_ref.at[me, mine], z_send.at[d], z_recv.at[t], {"tensor": o}))
    go(remote(unit_ref.at[mine], w_ref.at[me, mine], y_send.at[n_tensor - 1], y_recv.at[t], y_peer))
    go(remote(unit_ref, w_ref.at[me], c_send.at[0], c_recv.at[at(0, t)], c_peer))
    locals_ = [pltpu.make_async_copy(unit_ref, w_ref.at[me], own_sem.at[1])]
    for i, ref in enumerate((tok_ref, cot_ref)):
        locals_.append(pltpu.make_async_copy(ref.at[chunk(t)], acts_ref.at[i, t], own_sem.at[2 + i]))
    for copy in locals_:
        copy.start()

    arrived(w_ref.at[at(f_y, t), mine], y_recv.at[t])
    part = w_ref.at[at(f_y, t), mine]
    go(remote(part, part, x_send.at[0], x_recv.at[at(1, t)], x_peer))
    for d, o in enumerate(others):
        part = w_ref.at[at(f, o), mine]
        arrived(part, z_recv.at[o])
        if d == 1:
            go(remote(part, part, z_send.at[2], z_recv.at[o], {"tensor": pair}))
        go(remote(part, part, y_send.at[d], y_recv.at[o], y_peer))
        go(remote(part, part, x_send.at[1 + d], x_recv.at[at(0, o)], x_peer))
        if d == 1:
            share_acts()
    for d, o in enumerate(others):
        part = w_ref.at[at(f_y, o), mine]
        arrived(part, y_recv.at[o])
        go(remote(part, part, x_send.at[n_tensor + d], x_recv.at[at(1, o)], x_peer))
    part = w_ref.at[at(f_y, t)]
    arrived(w_ref.at[at(f_y, t), theirs], x_recv.at[at(1, t)])
    go(remote(part, part, c_send.at[1], c_recv.at[at(1, t)], c_peer))
    for k, ff in enumerate((f, f_y)):
        for d, o in enumerate(others):
            part = w_ref.at[at(ff, o)]
            arrived(w_ref.at[at(ff, o), theirs], x_recv.at[at(k, o)])
            go(remote(part, part, c_send.at[2 + k * (n_tensor - 1) + d], c_recv.at[at(k, o)], c_peer))
    for k, ff in enumerate((f_core, f_diag)):
        for o in [t] + others:
            arrived(w_ref.at[at(ff, o)], c_recv.at[at(k, o)])
    for o in others:
        for i in range(2):
            arrived(acts_ref.at[i, o], a_recv.at[2 * o + i])
    for copy in locals_:
        copy.wait()
    for copy in sends:
        copy.wait_send()


def bring(n_fsdp, n_tensor, unit, tokens, cotangent):
    tok_count, feats = tokens.shape
    anywhere = pl.BlockSpec(memory_space=pl.ANY)
    sem = pltpu.SemaphoreType.DMA
    return pl.pallas_call(
        functools.partial(bring_kernel, n_tensor),
        out_shape=(
            jax.ShapeDtypeStruct((n_fsdp * n_tensor,) + unit.shape, unit.dtype),
            jax.ShapeDtypeStruct((2, n_tensor, tok_count // n_tensor, feats), tokens.dtype),
        ),
        in_specs=[anywhere] * 3,
        out_specs=(anywhere,) * 2,
        scratch_shapes=[
            sem((n_tensor - 1,)), sem((n_tensor,)), sem((2 * n_tensor - 1,)), sem((2 * n_tensor,)), sem((2 * n_tensor - 2,)),
            sem((n_tensor,)), sem((n_tensor,)), sem((2 * n_tensor,)), sem((2 * n_tensor,)), sem((2 * n_tensor,)), sem((4,)),
        ],
        compiler_params=pltpu.CompilerParams(collective_id=0, has_side_effects=True),
    )(unit, tokens, cotangent)


def return_kernel(
    n_tensor, y_ref, left_ref, right_ref, out_ref, back_ref, gate_ref, up_ref, down_ref,
    c_out, c_buf, y_out, y_buf, z_out, z_buf, c_send, y_send, z_send, a_send, c_recv, y_recv, z_recv, a_recv, own_sem,
):
    f, t = lax.axis_index("fsdp"), lax.axis_index("tensor")
    f_core = f + 1 - 2 * lax.rem(f, 2)
    f_y = lax.rem(f + 2, 4)
    f_diag = f_core + f_y - f
    pair = t + 1 - 2 * lax.rem(t, 2)
    far = n_tensor - 1 - t
    y_peer, c_peer, pair_peer, far_peer = {"fsdp": f_y}, {"fsdp": f_core}, {"tensor": pair}, {"tensor": far}
    others = [n_tensor - 1 - pair, far, pair]
    order = others + [t]
    greet([{"tensor": o} for o in others] + [y_peer, c_peer])

    rows = y_ref.shape[2]
    pieces = left_ref.shape[1]
    mine = pl.ds(pl.multiple_of(t * rows, 16), rows)
    outs = (out_ref, back_ref)
    sends = []

    def at(ff, tt):
        return ff * n_tensor + tt

    def go(copy):
        copy.start()
        sends.append(copy)

    def arrived(view, sem):
        remote(view, view, own_sem.at[2], sem, c_peer).wait_recv()

    for d, o in enumerate(others):
        for i in range(2):
            go(remote(y_ref.at[i, o], outs[i].at[mine], a_send.at[2 * d + i], a_recv.at[2 * t + i], {"tensor": o}))
    locals_ = [pltpu.make_async_copy(y_ref.at[i, t], outs[i].at[mine], own_sem.at[i]) for i in range(2)]
    for copy in locals_:
        copy.start()

    def total(unit, j, *parts):
        own = lax.dot_general(
            left_ref[unit, j], right_ref[unit, j], (((0,), (0,)), ((), ())), preferred_element_type=jnp.float32
        )
        return sum([ref[i, j].astype(jnp.float32) for ref, i in parts], own)

    def fill(dst, slot, unit, *parts):
        @pl.loop(0, pieces)
        def _(j):
            dst[slot, j] = total(unit, j, *parts).astype(dst.dtype)

    for k, ff in ((1, f_diag), (0, f_core)):
        for d, o in enumerate(order):
            fill(c_out, at(k, d), at(ff, o))
            go(remote(c_out.at[at(k, d)], c_buf.at[at(k, d)], c_send.at[at(k, d)], c_recv.at[at(k, d)], c_peer))
        if k == 1:
            for d, o in enumerate(order):
                arrived(c_buf.at[at(1, d)], c_recv.at[at(1, d)])
                fill(y_out, d, at(f_y, o), (c_buf, at(1, d)))
                go(remote(y_out.at[d], y_buf.at[d], y_send.at[d], y_recv.at[d], y_peer))

    def near(d):
        arrived(c_buf.at[at(0, d)], c_recv.at[at(0, d)])
        arrived(y_buf.at[d], y_recv.at[d])
        return (c_buf, at(0, d)), (y_buf, d)

    for slot, (d, peer) in enumerate(((0, pair_peer), (2, pair_peer), (1, far_peer))):
        parts = near(d)
        if slot == 2:
            arrived(z_buf.at[0], z_recv.at[0])
            parts = parts + ((z_buf, 0),)
        fill(z_out, slot, at(f, order[d]), *parts)
        go(remote(z_out.at[slot], z_buf.at[slot], z_send.at[slot], z_recv.at[slot], peer))
    parts = near(3) + ((z_buf, 1), (z_buf, 2))
    arrived(z_buf.at[1], z_recv.at[1])
    arrived(z_buf.at[2], z_recv.at[2])
    per_share = pieces // 3
    for m, ref in enumerate((gate_ref, up_ref, down_ref)):
        for k in range(per_share):
            ref[0, k] = total(at(f, t), m * per_share + k, *parts).astype(ref.dtype)
    for o in others:
        for i in range(2):
            spot = pl.ds(pl.multiple_of(o * rows, 16), rows)
            arrived(outs[i].at[spot], a_recv.at[2 * o + i])
    for copy in locals_:
        copy.wait()
    for copy in sends:
        copy.wait_send()


def send_back(n_tensor, y, lefts, rights):
    rows, feats = y.shape[2:]
    pieces, _, side = lefts.shape[1:]
    anywhere, vmem = pl.BlockSpec(memory_space=pl.ANY), pl.BlockSpec(memory_space=pltpu.VMEM)
    sem = pltpu.SemaphoreType.DMA
    big = jax.ShapeDtypeStruct((n_tensor * rows, feats), y.dtype)
    small = jax.ShapeDtypeStruct((1, pieces // 3, side, side), y.dtype)

    def buf(count):
        return pltpu.VMEM((count, pieces, side, side), y.dtype)

    return pl.pallas_call(
        functools.partial(return_kernel, n_tensor),
        out_shape=(big, big, small, small, small),
        in_specs=[anywhere, vmem, vmem],
        out_specs=(anywhere, anywhere, vmem, vmem, vmem),
        scratch_shapes=[
            buf(2 * n_tensor), buf(2 * n_tensor), buf(n_tensor), buf(n_tensor), buf(n_tensor - 1), buf(n_tensor - 1),
            sem((2 * n_tensor,)), sem((n_tensor,)), sem((n_tensor - 1,)), sem((2 * n_tensor - 2,)),
            sem((2 * n_tensor,)), sem((n_tensor,)), sem((n_tensor - 1,)), sem((2 * n_tensor,)), sem((3,)),
        ],
        compiler_params=pltpu.CompilerParams(
            collective_id=1, has_side_effects=True, vmem_limit_bytes=40 * 1024 * 1024
        ),
    )(y, lefts, rights)


def solution(mesh):
    n_fsdp, n_tensor = mesh.shape["fsdp"], mesh.shape["tensor"]

    def on_device(*args):
        block_bytes = 3 * args[2].size * args[2].dtype.itemsize * n_fsdp * n_tensor
        known = mesh.shape["group"] == 2 and n_fsdp == 4 and n_tensor == 4
        if known and block_bytes <= 8 * 1024 * 1024 and args[0].shape[0] % (16 * n_tensor) == 0:
            return spread_plan(n_fsdp, n_tensor, *args)
        return gathered_plan(*args)

    in_specs = (
        P(("group", "fsdp"), "tensor"),
        P(("group", "fsdp"), "tensor"),
        P("tensor", "fsdp", None, None),
        P("tensor", "fsdp", None, None),
        P("tensor", "fsdp", None, None),
        P(None, "tensor", None),
        P(None, "tensor", None),
    )
    out_specs = (
        P(("group", "fsdp"), "tensor"),
        P(("group", "fsdp"), "tensor"),
        P(("group", "tensor"), "fsdp", None, None),
        P(("group", "tensor"), "fsdp", None, None),
        P(("group", "tensor"), "fsdp", None, None),
    )
    return jax.shard_map(
        on_device, mesh=mesh, in_specs=in_specs, out_specs=out_specs, check_vma=False
    )
```

```python
import functools

import jax
import jax.numpy as jnp
from jax import lax
from jax.experimental import pallas as pl
from jax.experimental.pallas import tpu as pltpu
from jax.sharding import PartitionSpec as P

finest = lax.Precision.HIGHEST


def slot_columns(counts, slot_count):
    running = jnp.cumsum(counts)
    places = lax.broadcasted_iota(jnp.int32, (slot_count, counts.shape[0]), 0)
    return jnp.sum((running[None, :] <= places).astype(jnp.int32), axis=1)


def slot_tables(slot_rows, counts, feature_count):
    slot_count = slot_rows.shape[0]
    col_width = counts.shape[0]
    columns = slot_columns(counts, slot_count)
    col_hot = (
        columns[:, None] == lax.broadcasted_iota(jnp.int32, (slot_count, col_width), 1)
    ).astype(jnp.float32)
    row_hot = (
        slot_rows[:, None] == lax.broadcasted_iota(jnp.int32, (slot_count, feature_count), 1)
    ).astype(jnp.float32)
    is_live = columns < col_width
    picker = jnp.minimum(columns, col_width - 1)
    return (col_hot, row_hot, is_live, picker)


def into_columns(terms, col_hot):
    return jnp.einsum("tsn,sc->tcn", terms, col_hot, precision=finest)


def into_rows(terms, row_hot):
    return jnp.einsum("tsk,sr->trk", terms, row_hot, precision=finest)


def pick_columns(values, picker, is_live):
    chosen = jnp.take(values, picker, axis=1)
    return jnp.where(is_live[None, :, None], chosen, jnp.zeros_like(chosen))


def gathered_plan(tokens, cotangent, gate_blocks, up_blocks, down_blocks, block_rows, col_counts):
    full_tokens = lax.all_gather(tokens, "tensor", axis=1, tiled=True)
    gate_w, up_w = (
        lax.all_gather(gate_blocks[0], "fsdp", axis=0, tiled=True),
        lax.all_gather(up_blocks[0], "fsdp", axis=0, tiled=True),
    )
    slot_rows = block_rows[:, 0, :]
    counts = col_counts[:, 0, :]
    tok_count = full_tokens.shape[0]
    side = gate_w.shape[-1]
    feature_count = full_tokens.shape[1] // side
    token_blocks = full_tokens.reshape(tok_count, feature_count, side)
    gate_tab = slot_tables(slot_rows[0], counts[0], feature_count)
    up_tab = slot_tables(slot_rows[1], counts[1], feature_count)
    down_tab = slot_tables(slot_rows[2], counts[2], feature_count)
    gate_in = jnp.take(token_blocks, slot_rows[0], axis=1)
    up_in = jnp.take(token_blocks, slot_rows[1], axis=1)
    gate_pre = into_columns(
        jnp.einsum("tsk,skn->tsn", gate_in, gate_w, preferred_element_type=jnp.float32), gate_tab[0]
    )
    up_pre = into_columns(
        jnp.einsum("tsk,skn->tsn", up_in, up_w, preferred_element_type=jnp.float32), up_tab[0]
    )
    sigma_gate = jax.nn.sigmoid(gate_pre)
    active = gate_pre * sigma_gate
    hidden = (active * up_pre).astype(jnp.bfloat16)
    down_w = lax.all_gather(down_blocks[0], "fsdp", axis=0, tiled=True)
    down_in = pick_columns(hidden, down_tab[3], down_tab[2])
    out_terms = jnp.einsum("tsn,snk->tsk", down_in, down_w, preferred_element_type=jnp.float32)
    out_part = into_rows(out_terms, down_tab[1]).reshape(tok_count, -1)
    layer_out = lax.psum_scatter(
        out_part.astype(jnp.bfloat16), "tensor", scatter_dimension=1, tiled=True
    )
    full_grads = lax.all_gather(cotangent, "tensor", axis=1, tiled=True)
    grad_blocks = full_grads.reshape(tok_count, feature_count, side)
    down_back = jnp.take(grad_blocks, slot_rows[2], axis=1)
    down_part = jnp.einsum("tsn,tsk->snk", down_in, down_back, preferred_element_type=jnp.float32)
    back_terms = jnp.einsum("tsk,snk->tsn", down_back, down_w, preferred_element_type=jnp.float32)
    dhidden = into_columns(back_terms, down_tab[0])
    dgate = (dhidden * up_pre * sigma_gate * (1.0 + gate_pre * (1.0 - sigma_gate))).astype(
        jnp.bfloat16
    )
    dup = (dhidden * active).astype(jnp.bfloat16)
    gate_back = pick_columns(dgate, gate_tab[3], gate_tab[2])
    up_back = pick_columns(dup, up_tab[3], up_tab[2])
    gate_terms = jnp.einsum("tsn,skn->tsk", gate_back, gate_w, preferred_element_type=jnp.float32)
    up_terms = jnp.einsum("tsn,skn->tsk", up_back, up_w, preferred_element_type=jnp.float32)
    in_part = (into_rows(gate_terms, gate_tab[1]) + into_rows(up_terms, up_tab[1])).reshape(
        tok_count, -1
    )
    input_grad = lax.psum_scatter(
        in_part.astype(jnp.bfloat16), "tensor", scatter_dimension=1, tiled=True
    )
    gate_part = jnp.einsum("tsk,tsn->skn", gate_in, gate_back, preferred_element_type=jnp.float32)
    up_part = jnp.einsum("tsk,tsn->skn", up_in, up_back, preferred_element_type=jnp.float32)
    gate_sum, up_sum, down_sum = (
        lax.psum_scatter(
            gate_part.astype(jnp.bfloat16), "fsdp", scatter_dimension=0, tiled=True
        ).astype(jnp.float32),
        lax.psum_scatter(
            up_part.astype(jnp.bfloat16), "fsdp", scatter_dimension=0, tiled=True
        ).astype(jnp.float32),
        lax.psum_scatter(
            down_part.astype(jnp.bfloat16), "fsdp", scatter_dimension=0, tiled=True
        ).astype(jnp.float32),
    )
    gate_grad = gate_sum.astype(jnp.bfloat16)[None]
    up_grad = up_sum.astype(jnp.bfloat16)[None]
    down_grad = down_sum.astype(jnp.bfloat16)[None]
    return (layer_out, input_grad, gate_grad, up_grad, down_grad)


def block_pass(slots, width, shares, meta_ref, acts_ref, w_ref, y_ref, left_ref, right_ref, gate, up, dhid, hid, dgate, dup, acc):
    n_tensor, tok, feats = acts_ref.shape[1:]
    side = w_ref.shape[-1]
    per_chunk = feats // side
    per_share = slots // shares
    trash, zero = width, width + 1

    def row_of(t, m, s):
        return meta_ref[t * 6 * slots + m * 2 * slots + s]

    def col_of(t, m, s, dead):
        col = meta_ref[t * 6 * slots + m * 2 * slots + slots + s]
        return jnp.where(col < width, col, dead)

    def act(which, row):
        lanes = pl.ds(pl.multiple_of(lax.rem(row, per_chunk) * side, side), side)
        return acts_ref[which, lax.div(row, per_chunk), :, lanes]

    def place(t, m, s):
        share, k = divmod(s, per_share)
        return share * n_tensor + t, pl.ds((m * per_share + k) * side, side)

    def weight(t, m, s):
        unit, rows = place(t, m, s)
        return w_ref[unit, rows, :]

    def dot(a, b, dims):
        return lax.dot_general(a, b, (dims, ((), ())), preferred_element_type=jnp.float32)

    plain, right_t = ((1,), (0,)), ((1,), (1,))
    acc[...] = jnp.zeros_like(acc)

    @pl.loop(0, n_tensor)
    def _(t):
        gate[...] = jnp.zeros_like(gate)
        up[...] = jnp.zeros_like(up)
        dhid[...] = jnp.zeros_like(dhid)
        for m, which, dims, into in ((0, 0, plain, gate), (1, 0, plain, up), (2, 1, right_t, dhid)):
            terms = [dot(act(which, row_of(t, m, s)), weight(t, m, s), dims) for s in range(slots)]
            for s in range(slots):
                into[col_of(t, m, s, trash)] += terms[s]

        @pl.loop(0, width)
        def _(c):
            g, u, d = gate[c], up[c], dhid[c]
            sig = jax.nn.sigmoid(g)
            active = g * sig
            hid[c] = (active * u).astype(hid.dtype)
            dgate[c] = (d * u * sig * (1.0 + g * (1.0 - sig))).astype(dgate.dtype)
            dup[c] = (d * active).astype(dup.dtype)

        for ref in (hid, dgate, dup):
            ref[zero] = jnp.zeros_like(ref[zero])

        for m, which, vals, dims, out in ((2, 1, hid, plain, 0), (0, 0, dgate, right_t, 1), (1, 0, dup, right_t, 1)):
            rows = [row_of(t, m, s) for s in range(slots)]
            picked = [vals[col_of(t, m, s, zero)] for s in range(slots)]
            terms = [dot(picked[s], weight(t, m, s), dims) for s in range(slots)]
            for s in range(slots):
                unit, at = s // per_share * n_tensor + t, m * per_share + s % per_share
                other = act(which, rows[s])
                pair = (picked[s], other) if m == 2 else (other, picked[s])
                left_ref[unit, at] = pair[0]
                right_ref[unit, at] = pair[1]
            for s in range(slots):
                acc[out, rows[s]] += terms[s]

    for out in range(2):
        for chunk in range(n_tensor):
            for j in range(per_chunk):
                y_ref[out, chunk, :, pl.ds(j * side, side)] = acc[out, chunk * per_chunk + j].astype(y_ref.dtype)


def run_blocks(meta, acts, weights, slots, width, shares):
    n_tensor, tok, feats = acts.shape[1:]
    units, _, side = weights.shape
    vmem = pl.BlockSpec(memory_space=pltpu.VMEM)
    picked = jax.ShapeDtypeStruct((units, 3 * slots // shares, tok, side), acts.dtype)
    cols = (width + 2, tok, side)
    return pl.pallas_call(
        functools.partial(block_pass, slots, width, shares),
        out_shape=(jax.ShapeDtypeStruct(acts.shape, acts.dtype), picked, picked),
        in_specs=[pl.BlockSpec(memory_space=pltpu.SMEM), vmem, vmem],
        out_specs=(vmem, vmem, vmem),
        scratch_shapes=[pltpu.VMEM(cols, jnp.float32)] * 3
        + [pltpu.VMEM(cols, jnp.bfloat16)] * 3
        + [pltpu.VMEM((2, n_tensor * feats // side, tok, side), jnp.float32)],
        compiler_params=pltpu.CompilerParams(vmem_limit_bytes=24 * 1024 * 1024),
    )(meta, acts, weights)


def pack_unit(gate_blocks, up_blocks, down_blocks, block_rows, col_counts):
    slots = block_rows.shape[-1]
    side = gate_blocks.shape[-1]
    cols = jax.vmap(lambda c: slot_columns(c, slots))(col_counts[:, 0, :])
    table = jnp.concatenate([block_rows[:, 0, :], cols], axis=1).reshape(-1)
    table = jnp.pad(table, (0, 32 * side - table.shape[0])).reshape(32, side)
    blocks = [b[0].reshape(-1, side) for b in (gate_blocks, up_blocks, down_blocks)]
    return jnp.concatenate(blocks + [table.astype(jnp.bfloat16)], axis=0)


def spread_plan(n_fsdp, n_tensor, tokens, cotangent, gate_blocks, up_blocks, down_blocks, block_rows, col_counts):
    slots, width = block_rows.shape[-1], col_counts.shape[-1]
    unit = pack_unit(gate_blocks, up_blocks, down_blocks, block_rows, col_counts)
    weights, acts = bring(n_fsdp, n_tensor, unit, tokens, cotangent)
    meta = weights[:n_tensor, -32:, :].astype(jnp.int32).reshape(n_tensor, -1)
    meta = meta[:, : 6 * slots].reshape(-1)
    y, lefts, rights = run_blocks(meta, acts, weights, slots, width, n_fsdp)
    return send_back(n_tensor, y, lefts, rights)


def greet(peers):
    barrier = pltpu.get_barrier_semaphore()
    for peer in peers:
        pl.semaphore_signal(barrier, inc=1, device_id=peer, device_id_type=pl.DeviceIdType.MESH)
    pl.semaphore_wait(barrier, len(peers))


def remote(src, dst, send_sem, recv_sem, peer):
    return pltpu.make_async_remote_copy(
        src_ref=src, dst_ref=dst, send_sem=send_sem, recv_sem=recv_sem,
        device_id=peer, device_id_type=pl.DeviceIdType.MESH,
    )


def bring_kernel(
    n_tensor, unit_ref, tok_ref, cot_ref, w_ref, acts_ref,
    z_send, y_send, x_send, c_send, a_send, z_recv, y_recv, x_recv, c_recv, a_recv, own_sem,
):
    group, f, t = (lax.axis_index(a) for a in ("group", "fsdp", "tensor"))
    f_core = f + 1 - 2 * lax.rem(f, 2)
    f_y = lax.rem(f + 2, 4)
    f_diag = f_core + f_y - f
    x_peer, y_peer, c_peer = {"group": 1 - group}, {"fsdp": f_y}, {"fsdp": f_core}
    pair = t + 1 - 2 * lax.rem(t, 2)
    far = n_tensor - 1 - t
    others = [pair, far, n_tensor - 1 - pair]
    greet([{"tensor": o} for o in others] + [x_peer, y_peer, c_peer])

    half = unit_ref.shape[0] // 2
    mine = pl.ds(pl.multiple_of(group * half, 16), half)
    theirs = pl.ds(pl.multiple_of((1 - group) * half, 16), half)
    rows = tok_ref.shape[0] // n_tensor

    def at(ff, tt):
        return ff * n_tensor + tt

    def chunk(tt):
        return pl.ds(pl.multiple_of(tt * rows, 16), rows)

    sends = []

    def go(copy):
        copy.start()
        sends.append(copy)

    def arrived(view, sem):
        remote(view, view, own_sem.at[0], sem, c_peer).wait_recv()

    def share_acts(i):
        ref = (tok_ref, cot_ref)[i]
        for d, o in enumerate(others):
            go(remote(ref.at[chunk(o)], acts_ref.at[i, t], a_send.at[2 * d + i], a_recv.at[2 * t + i], {"tensor": o}))

    me = at(f, t)
    for d, o in enumerate((far, pair)):
        go(remote(unit_ref.at[mine], w_ref.at[me, mine], z_send.at[d], z_recv.at[t], {"tensor": o}))
    go(remote(unit_ref, w_ref.at[me], y_send.at[n_tensor - 1], y_recv.at[t], y_peer))
    go(remote(unit_ref, w_ref.at[me], c_send.at[0], c_recv.at[at(0, t)], c_peer))
    locals_ = [pltpu.make_async_copy(unit_ref, w_ref.at[me], own_sem.at[1])]
    for i, ref in enumerate((tok_ref, cot_ref)):
        locals_.append(pltpu.make_async_copy(ref.at[chunk(t)], acts_ref.at[i, t], own_sem.at[2 + i]))
    for copy in locals_:
        copy.start()

    share_acts(0)
    for d, o in enumerate(others):
        part = w_ref.at[at(f, o), mine]
        arrived(part, z_recv.at[o])
        if d == 1:
            go(remote(part, part, z_send.at[2], z_recv.at[o], {"tensor": pair}))
        go(remote(part, part, y_send.at[d], y_recv.at[o], y_peer))
        go(remote(part, part, x_send.at[d], x_recv.at[at(0, o)], x_peer))
        if d == 1:
            share_acts(1)
    for d, o in enumerate(others):
        part = w_ref.at[at(f_y, o), mine]
        arrived(part, y_recv.at[o])
        go(remote(part, part, x_send.at[n_tensor - 1 + d], x_recv.at[at(1, o)], x_peer))
    part = w_ref.at[at(f_y, t)]
    arrived(part, y_recv.at[t])
    go(remote(part, part, c_send.at[1], c_recv.at[at(1, t)], c_peer))
    for k, ff in enumerate((f, f_y)):
        for d, o in enumerate(others):
            part = w_ref.at[at(ff, o)]
            arrived(w_ref.at[at(ff, o), theirs], x_recv.at[at(k, o)])
            go(remote(part, part, c_send.at[2 + k * (n_tensor - 1) + d], c_recv.at[at(k, o)], c_peer))
    for k, ff in enumerate((f_core, f_diag)):
        for o in [t] + others:
            arrived(w_ref.at[at(ff, o)], c_recv.at[at(k, o)])
    for o in others:
        for i in range(2):
            arrived(acts_ref.at[i, o], a_recv.at[2 * o + i])
    for copy in locals_:
        copy.wait()
    for copy in sends:
        copy.wait_send()


def bring(n_fsdp, n_tensor, unit, tokens, cotangent):
    tok_count, feats = tokens.shape
    anywhere = pl.BlockSpec(memory_space=pl.ANY)
    sem = pltpu.SemaphoreType.DMA
    return pl.pallas_call(
        functools.partial(bring_kernel, n_tensor),
        out_shape=(
            jax.ShapeDtypeStruct((n_fsdp * n_tensor,) + unit.shape, unit.dtype),
            jax.ShapeDtypeStruct((2, n_tensor, tok_count // n_tensor, feats), tokens.dtype),
        ),
        in_specs=[anywhere] * 3,
        out_specs=(anywhere,) * 2,
        scratch_shapes=[
            sem((n_tensor - 1,)), sem((n_tensor,)), sem((2 * n_tensor - 2,)), sem((2 * n_tensor,)), sem((2 * n_tensor - 2,)),
            sem((n_tensor,)), sem((n_tensor,)), sem((2 * n_tensor,)), sem((2 * n_tensor,)), sem((2 * n_tensor,)), sem((4,)),
        ],
        compiler_params=pltpu.CompilerParams(
            collective_id=0, has_side_effects=True, vmem_limit_bytes=2 * 1024 * 1024
        ),
    )(unit, tokens, cotangent)


def return_kernel(
    n_tensor, y_ref, left_ref, right_ref, out_ref, back_ref, gate_ref, up_ref, down_ref,
    c_out, c_buf, y_out, y_buf, z_out, z_buf, c_send, y_send, z_send, a_send, c_recv, y_recv, z_recv, a_recv, own_sem,
):
    f, t = lax.axis_index("fsdp"), lax.axis_index("tensor")
    f_core = f + 1 - 2 * lax.rem(f, 2)
    f_y = lax.rem(f + 2, 4)
    f_diag = f_core + f_y - f
    pair = t + 1 - 2 * lax.rem(t, 2)
    far = n_tensor - 1 - t
    y_peer, c_peer, pair_peer, far_peer = {"fsdp": f_y}, {"fsdp": f_core}, {"tensor": pair}, {"tensor": far}
    others = [n_tensor - 1 - pair, far, pair]
    order = others + [t]
    greet([{"tensor": o} for o in others] + [y_peer, c_peer])

    rows = y_ref.shape[2]
    pieces = left_ref.shape[1]
    mine = pl.ds(pl.multiple_of(t * rows, 16), rows)
    outs = (out_ref, back_ref)
    sends = []

    def at(ff, tt):
        return ff * n_tensor + tt

    def go(copy):
        copy.start()
        sends.append(copy)

    def arrived(view, sem):
        remote(view, view, own_sem.at[2], sem, c_peer).wait_recv()

    def share_out(i):
        for d, o in enumerate(others):
            go(remote(y_ref.at[i, o], outs[i].at[mine], a_send.at[2 * d + i], a_recv.at[2 * t + i], {"tensor": o}))

    share_out(0)
    locals_ = [pltpu.make_async_copy(y_ref.at[i, t], outs[i].at[mine], own_sem.at[i]) for i in range(2)]
    for copy in locals_:
        copy.start()

    def total(unit, j, *parts):
        own = lax.dot_general(
            left_ref[unit, j], right_ref[unit, j], (((0,), (0,)), ((), ())), preferred_element_type=jnp.float32
        )
        return sum([ref[i, j].astype(jnp.float32) for ref, i in parts], own)

    def fill(dst, slot, unit, *parts):
        @pl.loop(0, pieces)
        def _(j):
            dst[slot, j] = total(unit, j, *parts).astype(dst.dtype)

    for k, ff in ((1, f_diag), (0, f_core)):
        for d, o in enumerate(order):
            fill(c_out, at(k, d), at(ff, o))
            go(remote(c_out.at[at(k, d)], c_buf.at[at(k, d)], c_send.at[at(k, d)], c_recv.at[at(k, d)], c_peer))
        if k == 1:
            for d, o in enumerate(order):
                arrived(c_buf.at[at(1, d)], c_recv.at[at(1, d)])
                fill(y_out, d, at(f_y, o), (c_buf, at(1, d)))
                go(remote(y_out.at[d], y_buf.at[d], y_send.at[d], y_recv.at[d], y_peer))

    def near(d):
        arrived(c_buf.at[at(0, d)], c_recv.at[at(0, d)])
        arrived(y_buf.at[d], y_recv.at[d])
        return (c_buf, at(0, d)), (y_buf, d)

    for slot, (d, peer) in enumerate(((0, pair_peer), (2, pair_peer), (1, far_peer))):
        parts = near(d)
        if slot == 2:
            arrived(z_buf.at[0], z_recv.at[0])
            parts = parts + ((z_buf, 0),)
        fill(z_out, slot, at(f, order[d]), *parts)
        go(remote(z_out.at[slot], z_buf.at[slot], z_send.at[slot], z_recv.at[slot], peer))
        if slot == 0:
            share_out(1)
    parts = near(3) + ((z_buf, 1), (z_buf, 2))
    arrived(z_buf.at[1], z_recv.at[1])
    arrived(z_buf.at[2], z_recv.at[2])
    per_share = pieces // 3
    for m, ref in enumerate((gate_ref, up_ref, down_ref)):
        for k in range(per_share):
            ref[0, k] = total(at(f, t), m * per_share + k, *parts).astype(ref.dtype)
    for o in others:
        for i in range(2):
            spot = pl.ds(pl.multiple_of(o * rows, 16), rows)
            arrived(outs[i].at[spot], a_recv.at[2 * o + i])
    for copy in locals_:
        copy.wait()
    for copy in sends:
        copy.wait_send()


def send_back(n_tensor, y, lefts, rights):
    rows, feats = y.shape[2:]
    pieces, _, side = lefts.shape[1:]
    anywhere, vmem = pl.BlockSpec(memory_space=pl.ANY), pl.BlockSpec(memory_space=pltpu.VMEM)
    sem = pltpu.SemaphoreType.DMA
    big = jax.ShapeDtypeStruct((n_tensor * rows, feats), y.dtype)
    small = jax.ShapeDtypeStruct((1, pieces // 3, side, side), y.dtype)

    def buf(count):
        return pltpu.VMEM((count, pieces, side, side), y.dtype)

    return pl.pallas_call(
        functools.partial(return_kernel, n_tensor),
        out_shape=(big, big, small, small, small),
        in_specs=[anywhere, vmem, vmem],
        out_specs=(anywhere, anywhere, vmem, vmem, vmem),
        scratch_shapes=[
            buf(2 * n_tensor), buf(2 * n_tensor), buf(n_tensor), buf(n_tensor), buf(n_tensor - 1), buf(n_tensor - 1),
            sem((2 * n_tensor,)), sem((n_tensor,)), sem((n_tensor - 1,)), sem((2 * n_tensor - 2,)),
            sem((2 * n_tensor,)), sem((n_tensor,)), sem((n_tensor - 1,)), sem((2 * n_tensor,)), sem((3,)),
        ],
        compiler_params=pltpu.CompilerParams(
            collective_id=1, has_side_effects=True, vmem_limit_bytes=24 * 1024 * 1024
        ),
    )(y, lefts, rights)


def solution(mesh):
    n_fsdp, n_tensor = mesh.shape["fsdp"], mesh.shape["tensor"]

    def on_device(*args):
        block_bytes = 3 * args[2].size * args[2].dtype.itemsize * n_fsdp * n_tensor
        known = mesh.shape["group"] == 2 and n_fsdp == 4 and n_tensor == 4
        if known and block_bytes <= 8 * 1024 * 1024 and args[0].shape[0] % (16 * n_tensor) == 0:
            return spread_plan(n_fsdp, n_tensor, *args)
        return gathered_plan(*args)

    in_specs = (
        P(("group", "fsdp"), "tensor"),
        P(("group", "fsdp"), "tensor"),
        P("tensor", "fsdp", None, None),
        P("tensor", "fsdp", None, None),
        P("tensor", "fsdp", None, None),
        P(None, "tensor", None),
        P(None, "tensor", None),
    )
    out_specs = (
        P(("group", "fsdp"), "tensor"),
        P(("group", "fsdp"), "tensor"),
        P(("group", "tensor"), "fsdp", None, None),
        P(("group", "tensor"), "fsdp", None, None),
        P(("group", "tensor"), "fsdp", None, None),
    )
    return jax.shard_map(
        on_device, mesh=mesh, in_specs=in_specs, out_specs=out_specs, check_vma=False
    )
```

```python
import functools

import jax
import jax.numpy as jnp
from jax import lax
from jax.experimental import pallas as pl
from jax.experimental.pallas import tpu as pltpu
from jax.sharding import PartitionSpec as P

finest = lax.Precision.HIGHEST


def slot_columns(counts, slot_count):
    running = jnp.cumsum(counts)
    places = lax.broadcasted_iota(jnp.int32, (slot_count, counts.shape[0]), 0)
    return jnp.sum((running[None, :] <= places).astype(jnp.int32), axis=1)


def slot_tables(slot_rows, counts, feature_count):
    slot_count = slot_rows.shape[0]
    col_width = counts.shape[0]
    columns = slot_columns(counts, slot_count)
    col_hot = (
        columns[:, None] == lax.broadcasted_iota(jnp.int32, (slot_count, col_width), 1)
    ).astype(jnp.float32)
    row_hot = (
        slot_rows[:, None] == lax.broadcasted_iota(jnp.int32, (slot_count, feature_count), 1)
    ).astype(jnp.float32)
    is_live = columns < col_width
    picker = jnp.minimum(columns, col_width - 1)
    return (col_hot, row_hot, is_live, picker)


def into_columns(terms, col_hot):
    return jnp.einsum("tsn,sc->tcn", terms, col_hot, precision=finest)


def into_rows(terms, row_hot):
    return jnp.einsum("tsk,sr->trk", terms, row_hot, precision=finest)


def pick_columns(values, picker, is_live):
    chosen = jnp.take(values, picker, axis=1)
    return jnp.where(is_live[None, :, None], chosen, jnp.zeros_like(chosen))


def gathered_plan(tokens, cotangent, gate_blocks, up_blocks, down_blocks, block_rows, col_counts):
    full_tokens = lax.all_gather(tokens, "tensor", axis=1, tiled=True)
    gate_w, up_w = (
        lax.all_gather(gate_blocks[0], "fsdp", axis=0, tiled=True),
        lax.all_gather(up_blocks[0], "fsdp", axis=0, tiled=True),
    )
    slot_rows = block_rows[:, 0, :]
    counts = col_counts[:, 0, :]
    tok_count = full_tokens.shape[0]
    side = gate_w.shape[-1]
    feature_count = full_tokens.shape[1] // side
    token_blocks = full_tokens.reshape(tok_count, feature_count, side)
    gate_tab = slot_tables(slot_rows[0], counts[0], feature_count)
    up_tab = slot_tables(slot_rows[1], counts[1], feature_count)
    down_tab = slot_tables(slot_rows[2], counts[2], feature_count)
    gate_in = jnp.take(token_blocks, slot_rows[0], axis=1)
    up_in = jnp.take(token_blocks, slot_rows[1], axis=1)
    gate_pre = into_columns(
        jnp.einsum("tsk,skn->tsn", gate_in, gate_w, preferred_element_type=jnp.float32), gate_tab[0]
    )
    up_pre = into_columns(
        jnp.einsum("tsk,skn->tsn", up_in, up_w, preferred_element_type=jnp.float32), up_tab[0]
    )
    sigma_gate = jax.nn.sigmoid(gate_pre)
    active = gate_pre * sigma_gate
    hidden = (active * up_pre).astype(jnp.bfloat16)
    down_w = lax.all_gather(down_blocks[0], "fsdp", axis=0, tiled=True)
    down_in = pick_columns(hidden, down_tab[3], down_tab[2])
    out_terms = jnp.einsum("tsn,snk->tsk", down_in, down_w, preferred_element_type=jnp.float32)
    out_part = into_rows(out_terms, down_tab[1]).reshape(tok_count, -1)
    layer_out = lax.psum_scatter(
        out_part.astype(jnp.bfloat16), "tensor", scatter_dimension=1, tiled=True
    )
    full_grads = lax.all_gather(cotangent, "tensor", axis=1, tiled=True)
    grad_blocks = full_grads.reshape(tok_count, feature_count, side)
    down_back = jnp.take(grad_blocks, slot_rows[2], axis=1)
    down_part = jnp.einsum("tsn,tsk->snk", down_in, down_back, preferred_element_type=jnp.float32)
    back_terms = jnp.einsum("tsk,snk->tsn", down_back, down_w, preferred_element_type=jnp.float32)
    dhidden = into_columns(back_terms, down_tab[0])
    dgate = (dhidden * up_pre * sigma_gate * (1.0 + gate_pre * (1.0 - sigma_gate))).astype(
        jnp.bfloat16
    )
    dup = (dhidden * active).astype(jnp.bfloat16)
    gate_back = pick_columns(dgate, gate_tab[3], gate_tab[2])
    up_back = pick_columns(dup, up_tab[3], up_tab[2])
    gate_terms = jnp.einsum("tsn,skn->tsk", gate_back, gate_w, preferred_element_type=jnp.float32)
    up_terms = jnp.einsum("tsn,skn->tsk", up_back, up_w, preferred_element_type=jnp.float32)
    in_part = (into_rows(gate_terms, gate_tab[1]) + into_rows(up_terms, up_tab[1])).reshape(
        tok_count, -1
    )
    input_grad = lax.psum_scatter(
        in_part.astype(jnp.bfloat16), "tensor", scatter_dimension=1, tiled=True
    )
    gate_part = jnp.einsum("tsk,tsn->skn", gate_in, gate_back, preferred_element_type=jnp.float32)
    up_part = jnp.einsum("tsk,tsn->skn", up_in, up_back, preferred_element_type=jnp.float32)
    gate_sum, up_sum, down_sum = (
        lax.psum_scatter(
            gate_part.astype(jnp.bfloat16), "fsdp", scatter_dimension=0, tiled=True
        ).astype(jnp.float32),
        lax.psum_scatter(
            up_part.astype(jnp.bfloat16), "fsdp", scatter_dimension=0, tiled=True
        ).astype(jnp.float32),
        lax.psum_scatter(
            down_part.astype(jnp.bfloat16), "fsdp", scatter_dimension=0, tiled=True
        ).astype(jnp.float32),
    )
    gate_grad = gate_sum.astype(jnp.bfloat16)[None]
    up_grad = up_sum.astype(jnp.bfloat16)[None]
    down_grad = down_sum.astype(jnp.bfloat16)[None]
    return (layer_out, input_grad, gate_grad, up_grad, down_grad)


def block_pass(slots, width, shares, meta_ref, acts_hbm, w_hbm, y_ref, left_ref, right_ref, gate, up, dhid, hid, dgate, dup, acc, acts_ref, w_ref, acts_sem, w_sem):
    n_tensor, tok, feats = acts_hbm.shape[1:]

    def load(t, buf):
        return [
            pltpu.make_async_copy(w_hbm.at[share * n_tensor + t], w_ref.at[buf * shares + share], w_sem.at[buf, share])
            for share in range(shares)
        ]

    acts_copy = pltpu.make_async_copy(acts_hbm, acts_ref, acts_sem)
    acts_copy.start()
    for copy in load(0, 0):
        copy.start()
    side = w_ref.shape[-1]
    per_chunk = feats // side
    per_share = slots // shares
    trash, zero = width, width + 1

    def row_of(t, m, s):
        return meta_ref[t, m, s]

    def col_of(t, m, s, dead):
        col = meta_ref[t, 3 + m, s]
        return jnp.where(col < width, col, dead)

    def act(which, row):
        lanes = pl.ds(pl.multiple_of(lax.rem(row, per_chunk) * side, side), side)
        return acts_ref[which, lax.div(row, per_chunk), :, lanes]

    def place(t, m, s):
        share, k = divmod(s, per_share)
        return lax.rem(t, 2) * shares + share, pl.ds((m * per_share + k) * side, side)

    def weight(t, m, s):
        unit, rows = place(t, m, s)
        return w_ref[unit, rows, :]

    def dot(a, b, dims):
        return lax.dot_general(a, b, (dims, ((), ())), preferred_element_type=jnp.float32)

    plain, right_t = ((1,), (0,)), ((1,), (1,))
    acc[...] = jnp.zeros_like(acc)
    acts_copy.wait()

    @pl.loop(0, n_tensor)
    def _(t):
        gate[...] = jnp.zeros_like(gate)
        up[...] = jnp.zeros_like(up)
        dhid[...] = jnp.zeros_like(dhid)
        for copy in load(t, lax.rem(t, 2)):
            copy.wait()

        @pl.when(t + 1 < n_tensor)
        def _():
            for copy in load(t + 1, lax.rem(t + 1, 2)):
                copy.start()

        for m, which, dims, into in ((0, 0, plain, gate), (1, 0, plain, up), (2, 1, right_t, dhid)):
            terms = [dot(act(which, row_of(t, m, s)), weight(t, m, s), dims) for s in range(slots)]
            for s in range(slots):
                into[col_of(t, m, s, trash)] += terms[s]

        @pl.loop(0, width)
        def _(c):
            g, u, d = gate[c], up[c], dhid[c]
            sig = jax.nn.sigmoid(g)
            active = g * sig
            hid[c] = (active * u).astype(hid.dtype)
            dgate[c] = (d * u * sig * (1.0 + g * (1.0 - sig))).astype(dgate.dtype)
            dup[c] = (d * active).astype(dup.dtype)

        for ref in (hid, dgate, dup):
            ref[zero] = jnp.zeros_like(ref[zero])

        for m, which, vals, dims, out in ((2, 1, hid, plain, 0), (0, 0, dgate, right_t, 1), (1, 0, dup, right_t, 1)):
            rows = [row_of(t, m, s) for s in range(slots)]
            picked = [vals[col_of(t, m, s, zero)] for s in range(slots)]
            terms = [dot(picked[s], weight(t, m, s), dims) for s in range(slots)]
            for s in range(slots):
                unit, at = s // per_share * n_tensor + t, m * per_share + s % per_share
                other = act(which, rows[s])
                pair = (picked[s], other) if m == 2 else (other, picked[s])
                left_ref[unit, at] = pair[0]
                right_ref[unit, at] = pair[1]
            for s in range(slots):
                acc[out, rows[s]] += terms[s]

    for out in range(2):
        for chunk in range(n_tensor):
            for j in range(per_chunk):
                y_ref[out, chunk, :, pl.ds(j * side, side)] = acc[out, chunk * per_chunk + j].astype(y_ref.dtype)


def run_blocks(meta, acts, weights, slots, width, shares):
    n_tensor, tok, feats = acts.shape[1:]
    units, _, side = weights.shape
    vmem = pl.BlockSpec(memory_space=pltpu.VMEM)
    picked = jax.ShapeDtypeStruct((units, 3 * slots // shares, tok, side), acts.dtype)
    cols = (width + 2, tok, side)
    return pl.pallas_call(
        functools.partial(block_pass, slots, width, shares),
        out_shape=(jax.ShapeDtypeStruct(acts.shape, acts.dtype), picked, picked),
        in_specs=[pl.BlockSpec(memory_space=pltpu.SMEM)] + [pl.BlockSpec(memory_space=pl.ANY)] * 2,
        out_specs=(vmem, vmem, vmem),
        scratch_shapes=[pltpu.VMEM(cols, jnp.float32)] * 3
        + [pltpu.VMEM(cols, jnp.bfloat16)] * 3
        + [
            pltpu.VMEM((2, n_tensor * feats // side, tok, side), jnp.float32),
            pltpu.VMEM(acts.shape, acts.dtype),
            pltpu.VMEM((2 * shares,) + weights.shape[1:], weights.dtype),
            pltpu.SemaphoreType.DMA,
            pltpu.SemaphoreType.DMA((2, shares)),
        ],
        compiler_params=pltpu.CompilerParams(vmem_limit_bytes=24 * 1024 * 1024),
    )(meta, acts, weights)


def spread_plan(n_fsdp, n_tensor, tokens, cotangent, gate_blocks, up_blocks, down_blocks, block_rows, col_counts):
    slots, width = block_rows.shape[-1], col_counts.shape[-1]
    blocks = (gate_blocks[0], up_blocks[0], down_blocks[0])
    weights, acts, meta = bring(n_fsdp, n_tensor, blocks, tokens, cotangent, block_rows, col_counts)
    y, lefts, rights = run_blocks(meta, acts, weights, slots, width, n_fsdp)
    return send_back(n_tensor, y, lefts, rights)


def greet(peers):
    barrier = pltpu.get_barrier_semaphore()
    for peer in peers:
        pl.semaphore_signal(barrier, inc=1, device_id=peer, device_id_type=pl.DeviceIdType.MESH)
    pl.semaphore_wait(barrier, len(peers))


def remote(src, dst, send_sem, recv_sem, peer):
    return pltpu.make_async_remote_copy(
        src_ref=src, dst_ref=dst, send_sem=send_sem, recv_sem=recv_sem,
        device_id=peer, device_id_type=pl.DeviceIdType.MESH,
    )


def bring_kernel(
    n_tensor, gate_ref, up_ref, down_ref, tok_ref, cot_ref, rows_ref, counts_ref, w_ref, acts_ref, tables_ref, table,
    z_send, y_send, x_send, c_send, a_send, z_recv, y_recv, x_recv, c_recv, a_recv, t_send, t_recv, own_sem,
):
    group, f, t = (lax.axis_index(a) for a in ("group", "fsdp", "tensor"))
    f_core = f + 1 - 2 * lax.rem(f, 2)
    f_y = lax.rem(f + 2, 4)
    f_diag = f_core + f_y - f
    x_peer, y_peer, c_peer = {"group": 1 - group}, {"fsdp": f_y}, {"fsdp": f_core}
    pair = t + 1 - 2 * lax.rem(t, 2)
    far = n_tensor - 1 - t
    others = [pair, far, n_tensor - 1 - pair]
    me = f * n_tensor + t
    part_rows = gate_ref.shape[0]
    blocks = [
        pltpu.make_async_copy(ref, w_ref.at[me, pl.ds(m * part_rows, part_rows)], own_sem.at[4 + m])
        for m, ref in enumerate((gate_ref, up_ref, down_ref))
    ]
    for copy in blocks:
        copy.start()
    greet([{"tensor": o} for o in others] + [x_peer, y_peer, c_peer])
    for copy in blocks:
        copy.wait()

    unit_ref = w_ref.at[me]
    half = w_ref.shape[1] // 2
    mine = pl.ds(pl.multiple_of(group * half, 16), half)
    theirs = pl.ds(pl.multiple_of((1 - group) * half, 16), half)
    rows = tok_ref.shape[0] // n_tensor

    def at(ff, tt):
        return ff * n_tensor + tt

    def chunk(tt):
        return pl.ds(pl.multiple_of(tt * rows, 16), rows)

    sends = []

    def go(copy):
        copy.start()
        sends.append(copy)

    def arrived(view, sem):
        remote(view, view, own_sem.at[0], sem, c_peer).wait_recv()

    def share_acts(i):
        ref = (tok_ref, cot_ref)[i]
        for d, o in enumerate(others):
            go(remote(ref.at[chunk(o)], acts_ref.at[i, t], a_send.at[2 * d + i], a_recv.at[2 * t + i], {"tensor": o}))

    for d, o in enumerate((far, pair)):
        go(remote(w_ref.at[me, mine], w_ref.at[me, mine], z_send.at[d], z_recv.at[t], {"tensor": o}))
    go(remote(unit_ref, w_ref.at[me], y_send.at[n_tensor - 1], y_recv.at[t], y_peer))
    go(remote(unit_ref, w_ref.at[me], c_send.at[0], c_recv.at[at(0, t)], c_peer))
    slots, width = rows_ref.shape[-1], counts_ref.shape[-1]
    lanes = table.shape[-1]
    lower = lax.broadcasted_iota(jnp.int32, (width, width), 0) >= lax.broadcasted_iota(jnp.int32, (width, width), 1)
    places = lax.broadcasted_iota(jnp.int32, (width, lanes), 1)
    table[...] = jnp.zeros_like(table)
    for m in range(3):
        running = jnp.sum(jnp.where(lower, counts_ref[m], 0), axis=1, keepdims=True)
        table[pl.ds(m, 1), pl.ds(0, slots)] = rows_ref[m]
        table[pl.ds(3 + m, 1), :] = jnp.sum((running <= places).astype(jnp.int32), axis=0, keepdims=True)
    for d, o in enumerate(others):
        go(remote(table, tables_ref.at[t], t_send.at[d], t_recv.at[t], {"tensor": o}))
    locals_ = [pltpu.make_async_copy(table, tables_ref.at[t], own_sem.at[1])]
    for i, ref in enumerate((tok_ref, cot_ref)):
        locals_.append(pltpu.make_async_copy(ref.at[chunk(t)], acts_ref.at[i, t], own_sem.at[2 + i]))
    for copy in locals_:
        copy.start()

    for d, o in enumerate(others):
        part = w_ref.at[at(f, o), mine]
        arrived(part, z_recv.at[o])
        if d == 1:
            go(remote(part, part, z_send.at[2], z_recv.at[o], {"tensor": pair}))
        go(remote(part, part, y_send.at[d], y_recv.at[o], y_peer))
        go(remote(part, part, x_send.at[d], x_recv.at[at(0, o)], x_peer))
        if d == 1:
            share_acts(0)
            share_acts(1)
    for d, o in enumerate(others):
        part = w_ref.at[at(f_y, o), mine]
        arrived(part, y_recv.at[o])
        go(remote(part, part, x_send.at[n_tensor - 1 + d], x_recv.at[at(1, o)], x_peer))
    part = w_ref.at[at(f_y, t)]
    arrived(part, y_recv.at[t])
    go(remote(part, part, c_send.at[1], c_recv.at[at(1, t)], c_peer))
    for k, ff in enumerate((f, f_y)):
        for d, o in enumerate(others):
            part = w_ref.at[at(ff, o)]
            arrived(w_ref.at[at(ff, o), theirs], x_recv.at[at(k, o)])
            go(remote(part, part, c_send.at[2 + k * (n_tensor - 1) + d], c_recv.at[at(k, o)], c_peer))
    for k, ff in enumerate((f_core, f_diag)):
        for o in [t] + others:
            arrived(w_ref.at[at(ff, o)], c_recv.at[at(k, o)])
    for o in others:
        arrived(tables_ref.at[o], t_recv.at[o])
        for i in range(2):
            arrived(acts_ref.at[i, o], a_recv.at[2 * o + i])
    for copy in locals_:
        copy.wait()
    for copy in sends:
        copy.wait_send()


def bring(n_fsdp, n_tensor, blocks, tokens, cotangent, block_rows, col_counts):
    tok_count, feats = tokens.shape
    side = blocks[0].shape[-1]
    anywhere, vmem = pl.BlockSpec(memory_space=pl.ANY), pl.BlockSpec(memory_space=pltpu.VMEM)
    sem = pltpu.SemaphoreType.DMA
    parts = [b.reshape(-1, side) for b in blocks]
    unit_rows = 3 * parts[0].shape[0]
    return pl.pallas_call(
        functools.partial(bring_kernel, n_tensor),
        out_shape=(
            jax.ShapeDtypeStruct((n_fsdp * n_tensor, unit_rows, side), tokens.dtype),
            jax.ShapeDtypeStruct((2, n_tensor, tok_count // n_tensor, feats), tokens.dtype),
            jax.ShapeDtypeStruct((n_tensor, 8, 128), jnp.int32),
        ),
        in_specs=[anywhere] * 5 + [vmem] * 2,
        out_specs=(anywhere,) * 3,
        scratch_shapes=[
            pltpu.VMEM((8, 128), jnp.int32),
            sem((n_tensor - 1,)), sem((n_tensor,)), sem((2 * n_tensor - 2,)), sem((2 * n_tensor,)), sem((2 * n_tensor - 2,)),
            sem((n_tensor,)), sem((n_tensor,)), sem((2 * n_tensor,)), sem((2 * n_tensor,)), sem((2 * n_tensor,)),
            sem((n_tensor - 1,)), sem((n_tensor,)), sem((7,)),
        ],
        compiler_params=pltpu.CompilerParams(
            collective_id=0, has_side_effects=True, vmem_limit_bytes=56 * 1024 * 1024
        ),
    )(*parts, tokens, cotangent, block_rows, col_counts)


def return_kernel(
    n_tensor, y_ref, left_ref, right_ref, out_ref, back_ref, gate_ref, up_ref, down_ref,
    c_out, c_buf, y_out, y_buf, z_out, z_buf, c_send, y_send, z_send, a_send, c_recv, y_recv, z_recv, a_recv, own_sem,
):
    f, t = lax.axis_index("fsdp"), lax.axis_index("tensor")
    f_core = f + 1 - 2 * lax.rem(f, 2)
    f_y = lax.rem(f + 2, 4)
    f_diag = f_core + f_y - f
    pair = t + 1 - 2 * lax.rem(t, 2)
    far = n_tensor - 1 - t
    y_peer, c_peer, pair_peer, far_peer = {"fsdp": f_y}, {"fsdp": f_core}, {"tensor": pair}, {"tensor": far}
    others = [n_tensor - 1 - pair, far, pair]
    order = others + [t]
    greet([{"tensor": o} for o in others] + [y_peer, c_peer])

    rows = y_ref.shape[2]
    pieces = left_ref.shape[1]
    mine = pl.ds(pl.multiple_of(t * rows, 16), rows)
    outs = (out_ref, back_ref)
    sends = []

    def at(ff, tt):
        return ff * n_tensor + tt

    def go(copy):
        copy.start()
        sends.append(copy)

    def arrived(view, sem):
        remote(view, view, own_sem.at[2], sem, c_peer).wait_recv()

    def share_out(i):
        for d, o in enumerate(others):
            go(remote(y_ref.at[i, o], outs[i].at[mine], a_send.at[2 * d + i], a_recv.at[2 * t + i], {"tensor": o}))

    share_out(0)
    share_out(1)
    locals_ = [pltpu.make_async_copy(y_ref.at[i, t], outs[i].at[mine], own_sem.at[i]) for i in range(2)]
    for copy in locals_:
        copy.start()

    def total(unit, j, *parts):
        own = lax.dot_general(
            left_ref[unit, j], right_ref[unit, j], (((0,), (0,)), ((), ())), preferred_element_type=jnp.float32
        )
        return sum([ref[i, j].astype(jnp.float32) for ref, i in parts], own)

    def fill(dst, slot, unit, *parts):
        @pl.loop(0, pieces)
        def _(j):
            dst[slot, j] = total(unit, j, *parts).astype(dst.dtype)

    for k, ff in ((1, f_diag), (0, f_core)):
        for d, o in enumerate(order):
            fill(c_out, at(k, d), at(ff, o))
            go(remote(c_out.at[at(k, d)], c_buf.at[at(k, d)], c_send.at[at(k, d)], c_recv.at[at(k, d)], c_peer))
        if k == 1:
            for d, o in enumerate(order):
                arrived(c_buf.at[at(1, d)], c_recv.at[at(1, d)])
                fill(y_out, d, at(f_y, o), (c_buf, at(1, d)))
                go(remote(y_out.at[d], y_buf.at[d], y_send.at[d], y_recv.at[d], y_peer))

    def near(d):
        arrived(c_buf.at[at(0, d)], c_recv.at[at(0, d)])
        arrived(y_buf.at[d], y_recv.at[d])
        return (c_buf, at(0, d)), (y_buf, d)

    for slot, (d, peer) in enumerate(((0, pair_peer), (2, pair_peer), (1, far_peer))):
        parts = near(d)
        if slot == 2:
            arrived(z_buf.at[0], z_recv.at[0])
            parts = parts + ((z_buf, 0),)
        fill(z_out, slot, at(f, order[d]), *parts)
        go(remote(z_out.at[slot], z_buf.at[slot], z_send.at[slot], z_recv.at[slot], peer))
    parts = near(3) + ((z_buf, 1), (z_buf, 2))
    arrived(z_buf.at[1], z_recv.at[1])
    arrived(z_buf.at[2], z_recv.at[2])
    per_share = pieces // 3
    for m, ref in enumerate((gate_ref, up_ref, down_ref)):
        for k in range(per_share):
            ref[0, k] = total(at(f, t), m * per_share + k, *parts).astype(ref.dtype)
    for o in others:
        for i in range(2):
            spot = pl.ds(pl.multiple_of(o * rows, 16), rows)
            arrived(outs[i].at[spot], a_recv.at[2 * o + i])
    for copy in locals_:
        copy.wait()
    for copy in sends:
        copy.wait_send()


def send_back(n_tensor, y, lefts, rights):
    rows, feats = y.shape[2:]
    pieces, _, side = lefts.shape[1:]
    anywhere, vmem = pl.BlockSpec(memory_space=pl.ANY), pl.BlockSpec(memory_space=pltpu.VMEM)
    sem = pltpu.SemaphoreType.DMA
    big = jax.ShapeDtypeStruct((n_tensor * rows, feats), y.dtype)
    small = jax.ShapeDtypeStruct((1, pieces // 3, side, side), y.dtype)

    def buf(count):
        return pltpu.VMEM((count, pieces, side, side), y.dtype)

    return pl.pallas_call(
        functools.partial(return_kernel, n_tensor),
        out_shape=(big, big, small, small, small),
        in_specs=[anywhere, vmem, vmem],
        out_specs=(anywhere, anywhere, vmem, vmem, vmem),
        scratch_shapes=[
            buf(2 * n_tensor), buf(2 * n_tensor), buf(n_tensor), buf(n_tensor), buf(n_tensor - 1), buf(n_tensor - 1),
            sem((2 * n_tensor,)), sem((n_tensor,)), sem((n_tensor - 1,)), sem((2 * n_tensor - 2,)),
            sem((2 * n_tensor,)), sem((n_tensor,)), sem((n_tensor - 1,)), sem((2 * n_tensor,)), sem((3,)),
        ],
        compiler_params=pltpu.CompilerParams(
            collective_id=1, has_side_effects=True, vmem_limit_bytes=24 * 1024 * 1024
        ),
    )(y, lefts, rights)


def solution(mesh):
    n_fsdp, n_tensor = mesh.shape["fsdp"], mesh.shape["tensor"]

    def on_device(*args):
        block_bytes = 3 * args[2].size * args[2].dtype.itemsize * n_fsdp * n_tensor
        known = mesh.shape["group"] == 2 and n_fsdp == 4 and n_tensor == 4
        if known and block_bytes <= 8 * 1024 * 1024 and args[0].shape[0] % (16 * n_tensor) == 0:
            return spread_plan(n_fsdp, n_tensor, *args)
        return gathered_plan(*args)

    in_specs = (
        P(("group", "fsdp"), "tensor"),
        P(("group", "fsdp"), "tensor"),
        P("tensor", "fsdp", None, None),
        P("tensor", "fsdp", None, None),
        P("tensor", "fsdp", None, None),
        P(None, "tensor", None),
        P(None, "tensor", None),
    )
    out_specs = (
        P(("group", "fsdp"), "tensor"),
        P(("group", "fsdp"), "tensor"),
        P(("group", "tensor"), "fsdp", None, None),
        P(("group", "tensor"), "fsdp", None, None),
        P(("group", "tensor"), "fsdp", None, None),
    )
    return jax.shard_map(
        on_device, mesh=mesh, in_specs=in_specs, out_specs=out_specs, check_vma=False
    )
```

```python
import functools

import jax
import jax.numpy as jnp
from jax import lax
from jax.experimental import pallas as pl
from jax.experimental.pallas import tpu as pltpu
from jax.sharding import PartitionSpec as P

finest = lax.Precision.HIGHEST


def slot_columns(counts, slot_count):
    running = jnp.cumsum(counts)
    places = lax.broadcasted_iota(jnp.int32, (slot_count, counts.shape[0]), 0)
    return jnp.sum((running[None, :] <= places).astype(jnp.int32), axis=1)


def slot_tables(slot_rows, counts, feature_count):
    slot_count = slot_rows.shape[0]
    col_width = counts.shape[0]
    columns = slot_columns(counts, slot_count)
    col_hot = (
        columns[:, None] == lax.broadcasted_iota(jnp.int32, (slot_count, col_width), 1)
    ).astype(jnp.float32)
    row_hot = (
        slot_rows[:, None] == lax.broadcasted_iota(jnp.int32, (slot_count, feature_count), 1)
    ).astype(jnp.float32)
    is_live = columns < col_width
    picker = jnp.minimum(columns, col_width - 1)
    return (col_hot, row_hot, is_live, picker)


def into_columns(terms, col_hot):
    return jnp.einsum("tsn,sc->tcn", terms, col_hot, precision=finest)


def into_rows(terms, row_hot):
    return jnp.einsum("tsk,sr->trk", terms, row_hot, precision=finest)


def pick_columns(values, picker, is_live):
    chosen = jnp.take(values, picker, axis=1)
    return jnp.where(is_live[None, :, None], chosen, jnp.zeros_like(chosen))


def gathered_plan(tokens, cotangent, gate_blocks, up_blocks, down_blocks, block_rows, col_counts):
    full_tokens = lax.all_gather(tokens, "tensor", axis=1, tiled=True)
    gate_w, up_w = (
        lax.all_gather(gate_blocks[0], "fsdp", axis=0, tiled=True),
        lax.all_gather(up_blocks[0], "fsdp", axis=0, tiled=True),
    )
    slot_rows = block_rows[:, 0, :]
    counts = col_counts[:, 0, :]
    tok_count = full_tokens.shape[0]
    side = gate_w.shape[-1]
    feature_count = full_tokens.shape[1] // side
    token_blocks = full_tokens.reshape(tok_count, feature_count, side)
    gate_tab = slot_tables(slot_rows[0], counts[0], feature_count)
    up_tab = slot_tables(slot_rows[1], counts[1], feature_count)
    down_tab = slot_tables(slot_rows[2], counts[2], feature_count)
    gate_in = jnp.take(token_blocks, slot_rows[0], axis=1)
    up_in = jnp.take(token_blocks, slot_rows[1], axis=1)
    gate_pre = into_columns(
        jnp.einsum("tsk,skn->tsn", gate_in, gate_w, preferred_element_type=jnp.float32), gate_tab[0]
    )
    up_pre = into_columns(
        jnp.einsum("tsk,skn->tsn", up_in, up_w, preferred_element_type=jnp.float32), up_tab[0]
    )
    sigma_gate = jax.nn.sigmoid(gate_pre)
    active = gate_pre * sigma_gate
    hidden = (active * up_pre).astype(jnp.bfloat16)
    down_w = lax.all_gather(down_blocks[0], "fsdp", axis=0, tiled=True)
    down_in = pick_columns(hidden, down_tab[3], down_tab[2])
    out_terms = jnp.einsum("tsn,snk->tsk", down_in, down_w, preferred_element_type=jnp.float32)
    out_part = into_rows(out_terms, down_tab[1]).reshape(tok_count, -1)
    layer_out = lax.psum_scatter(
        out_part.astype(jnp.bfloat16), "tensor", scatter_dimension=1, tiled=True
    )
    full_grads = lax.all_gather(cotangent, "tensor", axis=1, tiled=True)
    grad_blocks = full_grads.reshape(tok_count, feature_count, side)
    down_back = jnp.take(grad_blocks, slot_rows[2], axis=1)
    down_part = jnp.einsum("tsn,tsk->snk", down_in, down_back, preferred_element_type=jnp.float32)
    back_terms = jnp.einsum("tsk,snk->tsn", down_back, down_w, preferred_element_type=jnp.float32)
    dhidden = into_columns(back_terms, down_tab[0])
    dgate = (dhidden * up_pre * sigma_gate * (1.0 + gate_pre * (1.0 - sigma_gate))).astype(
        jnp.bfloat16
    )
    dup = (dhidden * active).astype(jnp.bfloat16)
    gate_back = pick_columns(dgate, gate_tab[3], gate_tab[2])
    up_back = pick_columns(dup, up_tab[3], up_tab[2])
    gate_terms = jnp.einsum("tsn,skn->tsk", gate_back, gate_w, preferred_element_type=jnp.float32)
    up_terms = jnp.einsum("tsn,skn->tsk", up_back, up_w, preferred_element_type=jnp.float32)
    in_part = (into_rows(gate_terms, gate_tab[1]) + into_rows(up_terms, up_tab[1])).reshape(
        tok_count, -1
    )
    input_grad = lax.psum_scatter(
        in_part.astype(jnp.bfloat16), "tensor", scatter_dimension=1, tiled=True
    )
    gate_part = jnp.einsum("tsk,tsn->skn", gate_in, gate_back, preferred_element_type=jnp.float32)
    up_part = jnp.einsum("tsk,tsn->skn", up_in, up_back, preferred_element_type=jnp.float32)
    gate_sum, up_sum, down_sum = (
        lax.psum_scatter(
            gate_part.astype(jnp.bfloat16), "fsdp", scatter_dimension=0, tiled=True
        ).astype(jnp.float32),
        lax.psum_scatter(
            up_part.astype(jnp.bfloat16), "fsdp", scatter_dimension=0, tiled=True
        ).astype(jnp.float32),
        lax.psum_scatter(
            down_part.astype(jnp.bfloat16), "fsdp", scatter_dimension=0, tiled=True
        ).astype(jnp.float32),
    )
    gate_grad = gate_sum.astype(jnp.bfloat16)[None]
    up_grad = up_sum.astype(jnp.bfloat16)[None]
    down_grad = down_sum.astype(jnp.bfloat16)[None]
    return (layer_out, input_grad, gate_grad, up_grad, down_grad)


def block_pass(slots, width, shares, meta_ref, acts_hbm, w_hbm, y_ref, left_ref, right_ref, gate, up, dhid, hid, dgate, dup, acc, acts_ref, w_ref, acts_sem, w_sem):
    n_tensor, tok, feats = acts_hbm.shape[1:]

    def load(t, buf):
        return [
            pltpu.make_async_copy(w_hbm.at[share * n_tensor + t], w_ref.at[buf * shares + share], w_sem.at[buf, share])
            for share in range(shares)
        ]

    acts_copy = pltpu.make_async_copy(acts_hbm, acts_ref, acts_sem)
    acts_copy.start()
    for copy in load(0, 0):
        copy.start()
    side = w_ref.shape[-1]
    per_chunk = feats // side
    per_share = slots // shares
    trash, zero = width, width + 1

    def row_of(t, m, s):
        return meta_ref[t * 6 * slots + m * 2 * slots + s]

    def col_of(t, m, s, dead):
        col = meta_ref[t * 6 * slots + m * 2 * slots + slots + s]
        return jnp.where(col < width, col, dead)

    def act(which, row):
        lanes = pl.ds(pl.multiple_of(lax.rem(row, per_chunk) * side, side), side)
        return acts_ref[which, lax.div(row, per_chunk), :, lanes]

    def place(t, m, s):
        share, k = divmod(s, per_share)
        return lax.rem(t, 2) * shares + share, pl.ds((m * per_share + k) * side, side)

    def weight(t, m, s):
        unit, rows = place(t, m, s)
        return w_ref[unit, rows, :]

    def dot(a, b, dims):
        return lax.dot_general(a, b, (dims, ((), ())), preferred_element_type=jnp.float32)

    plain, right_t = ((1,), (0,)), ((1,), (1,))
    acc[...] = jnp.zeros_like(acc)
    acts_copy.wait()

    @pl.loop(0, n_tensor)
    def _(t):
        gate[...] = jnp.zeros_like(gate)
        up[...] = jnp.zeros_like(up)
        dhid[...] = jnp.zeros_like(dhid)
        for copy in load(t, lax.rem(t, 2)):
            copy.wait()

        @pl.when(t + 1 < n_tensor)
        def _():
            for copy in load(t + 1, lax.rem(t + 1, 2)):
                copy.start()

        for m, which, dims, into in ((0, 0, plain, gate), (1, 0, plain, up), (2, 1, right_t, dhid)):
            terms = [dot(act(which, row_of(t, m, s)), weight(t, m, s), dims) for s in range(slots)]
            for s in range(slots):
                into[col_of(t, m, s, trash)] += terms[s]

        @pl.loop(0, width)
        def _(c):
            g, u, d = gate[c], up[c], dhid[c]
            sig = jax.nn.sigmoid(g)
            active = g * sig
            hid[c] = (active * u).astype(hid.dtype)
            dgate[c] = (d * u * sig * (1.0 + g * (1.0 - sig))).astype(dgate.dtype)
            dup[c] = (d * active).astype(dup.dtype)

        for ref in (hid, dgate, dup):
            ref[zero] = jnp.zeros_like(ref[zero])

        for m, which, vals, dims, out in ((2, 1, hid, plain, 0), (0, 0, dgate, right_t, 1), (1, 0, dup, right_t, 1)):
            rows = [row_of(t, m, s) for s in range(slots)]
            picked = [vals[col_of(t, m, s, zero)] for s in range(slots)]
            terms = [dot(picked[s], weight(t, m, s), dims) for s in range(slots)]
            for s in range(slots):
                unit, at = s // per_share * n_tensor + t, m * per_share + s % per_share
                other = act(which, rows[s])
                pair = (picked[s], other) if m == 2 else (other, picked[s])
                left_ref[unit, at] = pair[0]
                right_ref[unit, at] = pair[1]
            for s in range(slots):
                acc[out, rows[s]] += terms[s]

    for out in range(2):
        for chunk in range(n_tensor):
            for j in range(per_chunk):
                y_ref[out, chunk, :, pl.ds(j * side, side)] = acc[out, chunk * per_chunk + j].astype(y_ref.dtype)


def run_blocks(meta, acts, weights, slots, width, shares):
    n_tensor, tok, feats = acts.shape[1:]
    units, _, side = weights.shape
    vmem = pl.BlockSpec(memory_space=pltpu.VMEM)
    picked = jax.ShapeDtypeStruct((units, 3 * slots // shares, tok, side), acts.dtype)
    cols = (width + 2, tok, side)
    return pl.pallas_call(
        functools.partial(block_pass, slots, width, shares),
        out_shape=(jax.ShapeDtypeStruct(acts.shape, acts.dtype), picked, picked),
        in_specs=[pl.BlockSpec(memory_space=pltpu.SMEM)] + [pl.BlockSpec(memory_space=pl.ANY)] * 2,
        out_specs=(vmem, vmem, vmem),
        scratch_shapes=[pltpu.VMEM(cols, jnp.float32)] * 3
        + [pltpu.VMEM(cols, jnp.bfloat16)] * 3
        + [
            pltpu.VMEM((2, n_tensor * feats // side, tok, side), jnp.float32),
            pltpu.VMEM(acts.shape, acts.dtype),
            pltpu.VMEM((2 * shares,) + weights.shape[1:], weights.dtype),
            pltpu.SemaphoreType.DMA,
            pltpu.SemaphoreType.DMA((2, shares)),
        ],
        compiler_params=pltpu.CompilerParams(vmem_limit_bytes=48 * 1024 * 1024),
    )(meta, acts, weights)


def pack_unit(gate_blocks, up_blocks, down_blocks, block_rows, col_counts):
    slots = block_rows.shape[-1]
    side = gate_blocks.shape[-1]
    cols = jax.vmap(lambda c: slot_columns(c, slots))(col_counts[:, 0, :])
    table = jnp.concatenate([block_rows[:, 0, :], cols], axis=1).reshape(-1)
    table = jnp.pad(table, (0, 32 * side - table.shape[0])).reshape(32, side)
    blocks = [b[0].reshape(-1, side) for b in (gate_blocks, up_blocks, down_blocks)]
    return jnp.concatenate(blocks + [table.astype(jnp.bfloat16)], axis=0)


def spread_plan(n_fsdp, n_tensor, tokens, cotangent, gate_blocks, up_blocks, down_blocks, block_rows, col_counts):
    slots, width = block_rows.shape[-1], col_counts.shape[-1]
    unit = pack_unit(gate_blocks, up_blocks, down_blocks, block_rows, col_counts)
    weights, acts = bring(n_fsdp, n_tensor, unit, tokens, cotangent)
    meta = weights[:n_tensor, -32:, :].astype(jnp.int32).reshape(n_tensor, -1)
    meta = meta[:, : 6 * slots].reshape(-1)
    y, lefts, rights = run_blocks(meta, acts, weights, slots, width, n_fsdp)
    return send_back(n_tensor, y, lefts, rights)


def greet(peers):
    barrier = pltpu.get_barrier_semaphore()
    for peer in peers:
        pl.semaphore_signal(barrier, inc=1, device_id=peer, device_id_type=pl.DeviceIdType.MESH)
    pl.semaphore_wait(barrier, len(peers))


def remote(src, dst, send_sem, recv_sem, peer):
    return pltpu.make_async_remote_copy(
        src_ref=src, dst_ref=dst, send_sem=send_sem, recv_sem=recv_sem,
        device_id=peer, device_id_type=pl.DeviceIdType.MESH,
    )


def bring_kernel(
    n_tensor, unit_ref, tok_ref, cot_ref, w_ref, acts_ref,
    z_send, y_send, x_send, c_send, a_send, z_recv, y_recv, x_recv, c_recv, a_recv, own_sem,
):
    group, f, t = (lax.axis_index(a) for a in ("group", "fsdp", "tensor"))
    f_core = f + 1 - 2 * lax.rem(f, 2)
    f_y = lax.rem(f + 2, 4)
    f_diag = f_core + f_y - f
    x_peer, y_peer, c_peer = {"group": 1 - group}, {"fsdp": f_y}, {"fsdp": f_core}
    pair = t + 1 - 2 * lax.rem(t, 2)
    far = n_tensor - 1 - t
    others = [pair, far, n_tensor - 1 - pair]
    greet([{"tensor": o} for o in others] + [x_peer, y_peer, c_peer])

    half = unit_ref.shape[0] // 2
    mine = pl.ds(pl.multiple_of(group * half, 16), half)
    theirs = pl.ds(pl.multiple_of((1 - group) * half, 16), half)
    rows = tok_ref.shape[0] // n_tensor

    def at(ff, tt):
        return ff * n_tensor + tt

    def chunk(tt):
        return pl.ds(pl.multiple_of(tt * rows, 16), rows)

    sends = []

    def go(copy):
        copy.start()
        sends.append(copy)

    def arrived(view, sem):
        remote(view, view, own_sem.at[0], sem, c_peer).wait_recv()

    def share_acts():
        for d, o in enumerate(others):
            for i, ref in enumerate((tok_ref, cot_ref)):
                go(remote(ref.at[chunk(o)], acts_ref.at[i, t], a_send.at[2 * d + i], a_recv.at[2 * t + i], {"tensor": o}))

    me = at(f, t)
    for d, o in enumerate((far, pair)):
        go(remote(unit_ref.at[mine], w_ref.at[me, mine], z_send.at[d], z_recv.at[t], {"tensor": o}))
    go(remote(unit_ref.at[mine], w_ref.at[me, mine], y_send.at[n_tensor - 1], y_recv.at[t], y_peer))
    go(remote(unit_ref, w_ref.at[me], c_send.at[0], c_recv.at[at(0, t)], c_peer))
    locals_ = [pltpu.make_async_copy(unit_ref, w_ref.at[me], own_sem.at[1])]
    for i, ref in enumerate((tok_ref, cot_ref)):
        locals_.append(pltpu.make_async_copy(ref.at[chunk(t)], acts_ref.at[i, t], own_sem.at[2 + i]))
    for copy in locals_:
        copy.start()

    arrived(w_ref.at[at(f_y, t), mine], y_recv.at[t])
    part = w_ref.at[at(f_y, t), mine]
    go(remote(part, part, x_send.at[0], x_recv.at[at(1, t)], x_peer))
    for d, o in enumerate(others):
        part = w_ref.at[at(f, o), mine]
        arrived(part, z_recv.at[o])
        if d == 1:
            go(remote(part, part, z_send.at[2], z_recv.at[o], {"tensor": pair}))
        go(remote(part, part, y_send.at[d], y_recv.at[o], y_peer))
        go(remote(part, part, x_send.at[1 + d], x_recv.at[at(0, o)], x_peer))
        if d == 1:
            share_acts()
    for d, o in enumerate(others):
        part = w_ref.at[at(f_y, o), mine]
        arrived(part, y_recv.at[o])
        go(remote(part, part, x_send.at[n_tensor + d], x_recv.at[at(1, o)], x_peer))
    part = w_ref.at[at(f_y, t)]
    arrived(w_ref.at[at(f_y, t), theirs], x_recv.at[at(1, t)])
    go(remote(part, part, c_send.at[1], c_recv.at[at(1, t)], c_peer))
    for k, ff in enumerate((f, f_y)):
        for d, o in enumerate(others):
            part = w_ref.at[at(ff, o)]
            arrived(w_ref.at[at(ff, o), theirs], x_recv.at[at(k, o)])
            go(remote(part, part, c_send.at[2 + k * (n_tensor - 1) + d], c_recv.at[at(k, o)], c_peer))
    for k, ff in enumerate((f_core, f_diag)):
        for o in [t] + others:
            arrived(w_ref.at[at(ff, o)], c_recv.at[at(k, o)])
    for o in others:
        for i in range(2):
            arrived(acts_ref.at[i, o], a_recv.at[2 * o + i])
    for copy in locals_:
        copy.wait()
    for copy in sends:
        copy.wait_send()


def bring(n_fsdp, n_tensor, unit, tokens, cotangent):
    tok_count, feats = tokens.shape
    anywhere = pl.BlockSpec(memory_space=pl.ANY)
    sem = pltpu.SemaphoreType.DMA
    return pl.pallas_call(
        functools.partial(bring_kernel, n_tensor),
        out_shape=(
            jax.ShapeDtypeStruct((n_fsdp * n_tensor,) + unit.shape, unit.dtype),
            jax.ShapeDtypeStruct((2, n_tensor, tok_count // n_tensor, feats), tokens.dtype),
        ),
        in_specs=[anywhere] * 3,
        out_specs=(anywhere,) * 2,
        scratch_shapes=[
            sem((n_tensor - 1,)), sem((n_tensor,)), sem((2 * n_tensor - 1,)), sem((2 * n_tensor,)), sem((2 * n_tensor - 2,)),
            sem((n_tensor,)), sem((n_tensor,)), sem((2 * n_tensor,)), sem((2 * n_tensor,)), sem((2 * n_tensor,)), sem((4,)),
        ],
        compiler_params=pltpu.CompilerParams(collective_id=0, has_side_effects=True),
    )(unit, tokens, cotangent)


def return_kernel(
    n_tensor, y_ref, left_ref, right_ref, out_ref, back_ref, gate_ref, up_ref, down_ref,
    c_out, c_buf, y_out, y_buf, z_out, z_buf, c_send, y_send, z_send, a_send, c_recv, y_recv, z_recv, a_recv, own_sem,
):
    f, t = lax.axis_index("fsdp"), lax.axis_index("tensor")
    f_core = f + 1 - 2 * lax.rem(f, 2)
    f_y = lax.rem(f + 2, 4)
    f_diag = f_core + f_y - f
    pair = t + 1 - 2 * lax.rem(t, 2)
    far = n_tensor - 1 - t
    y_peer, c_peer, pair_peer, far_peer = {"fsdp": f_y}, {"fsdp": f_core}, {"tensor": pair}, {"tensor": far}
    others = [n_tensor - 1 - pair, far, pair]
    order = others + [t]
    greet([{"tensor": o} for o in others] + [y_peer, c_peer])

    rows = y_ref.shape[2]
    pieces = left_ref.shape[1]
    mine = pl.ds(pl.multiple_of(t * rows, 16), rows)
    outs = (out_ref, back_ref)
    sends = []

    def at(ff, tt):
        return ff * n_tensor + tt

    def go(copy):
        copy.start()
        sends.append(copy)

    def arrived(view, sem):
        remote(view, view, own_sem.at[2], sem, c_peer).wait_recv()

    for d, o in enumerate(others):
        for i in range(2):
            go(remote(y_ref.at[i, o], outs[i].at[mine], a_send.at[2 * d + i], a_recv.at[2 * t + i], {"tensor": o}))
    locals_ = [pltpu.make_async_copy(y_ref.at[i, t], outs[i].at[mine], own_sem.at[i]) for i in range(2)]
    for copy in locals_:
        copy.start()

    def total(unit, j, *parts):
        own = lax.dot_general(
            left_ref[unit, j], right_ref[unit, j], (((0,), (0,)), ((), ())), preferred_element_type=jnp.float32
        )
        return sum([ref[i, j].astype(jnp.float32) for ref, i in parts], own)

    def fill(dst, slot, unit, *parts):
        @pl.loop(0, pieces)
        def _(j):
            dst[slot, j] = total(unit, j, *parts).astype(dst.dtype)

    for k, ff in ((1, f_diag), (0, f_core)):
        for d, o in enumerate(order):
            fill(c_out, at(k, d), at(ff, o))
            go(remote(c_out.at[at(k, d)], c_buf.at[at(k, d)], c_send.at[at(k, d)], c_recv.at[at(k, d)], c_peer))
        if k == 1:
            for d, o in enumerate(order):
                arrived(c_buf.at[at(1, d)], c_recv.at[at(1, d)])
                fill(y_out, d, at(f_y, o), (c_buf, at(1, d)))
                go(remote(y_out.at[d], y_buf.at[d], y_send.at[d], y_recv.at[d], y_peer))

    def near(d):
        arrived(c_buf.at[at(0, d)], c_recv.at[at(0, d)])
        arrived(y_buf.at[d], y_recv.at[d])
        return (c_buf, at(0, d)), (y_buf, d)

    for slot, (d, peer) in enumerate(((0, pair_peer), (2, pair_peer), (1, far_peer))):
        parts = near(d)
        if slot == 2:
            arrived(z_buf.at[0], z_recv.at[0])
            parts = parts + ((z_buf, 0),)
        fill(z_out, slot, at(f, order[d]), *parts)
        go(remote(z_out.at[slot], z_buf.at[slot], z_send.at[slot], z_recv.at[slot], peer))
    parts = near(3) + ((z_buf, 1), (z_buf, 2))
    arrived(z_buf.at[1], z_recv.at[1])
    arrived(z_buf.at[2], z_recv.at[2])
    per_share = pieces // 3
    for m, ref in enumerate((gate_ref, up_ref, down_ref)):
        for k in range(per_share):
            ref[0, k] = total(at(f, t), m * per_share + k, *parts).astype(ref.dtype)
    for o in others:
        for i in range(2):
            spot = pl.ds(pl.multiple_of(o * rows, 16), rows)
            arrived(outs[i].at[spot], a_recv.at[2 * o + i])
    for copy in locals_:
        copy.wait()
    for copy in sends:
        copy.wait_send()


def send_back(n_tensor, y, lefts, rights):
    rows, feats = y.shape[2:]
    pieces, _, side = lefts.shape[1:]
    anywhere, vmem = pl.BlockSpec(memory_space=pl.ANY), pl.BlockSpec(memory_space=pltpu.VMEM)
    sem = pltpu.SemaphoreType.DMA
    big = jax.ShapeDtypeStruct((n_tensor * rows, feats), y.dtype)
    small = jax.ShapeDtypeStruct((1, pieces // 3, side, side), y.dtype)

    def buf(count):
        return pltpu.VMEM((count, pieces, side, side), y.dtype)

    return pl.pallas_call(
        functools.partial(return_kernel, n_tensor),
        out_shape=(big, big, small, small, small),
        in_specs=[anywhere, vmem, vmem],
        out_specs=(anywhere, anywhere, vmem, vmem, vmem),
        scratch_shapes=[
            buf(2 * n_tensor), buf(2 * n_tensor), buf(n_tensor), buf(n_tensor), buf(n_tensor - 1), buf(n_tensor - 1),
            sem((2 * n_tensor,)), sem((n_tensor,)), sem((n_tensor - 1,)), sem((2 * n_tensor - 2,)),
            sem((2 * n_tensor,)), sem((n_tensor,)), sem((n_tensor - 1,)), sem((2 * n_tensor,)), sem((3,)),
        ],
        compiler_params=pltpu.CompilerParams(
            collective_id=1, has_side_effects=True, vmem_limit_bytes=24 * 1024 * 1024
        ),
    )(y, lefts, rights)


def solution(mesh):
    n_fsdp, n_tensor = mesh.shape["fsdp"], mesh.shape["tensor"]

    def on_device(*args):
        block_bytes = 3 * args[2].size * args[2].dtype.itemsize * n_fsdp * n_tensor
        known = mesh.shape["group"] == 2 and n_fsdp == 4 and n_tensor == 4
        if known and block_bytes <= 8 * 1024 * 1024 and args[0].shape[0] % (16 * n_tensor) == 0:
            return spread_plan(n_fsdp, n_tensor, *args)
        return gathered_plan(*args)

    in_specs = (
        P(("group", "fsdp"), "tensor"),
        P(("group", "fsdp"), "tensor"),
        P("tensor", "fsdp", None, None),
        P("tensor", "fsdp", None, None),
        P("tensor", "fsdp", None, None),
        P(None, "tensor", None),
        P(None, "tensor", None),
    )
    out_specs = (
        P(("group", "fsdp"), "tensor"),
        P(("group", "fsdp"), "tensor"),
        P(("group", "tensor"), "fsdp", None, None),
        P(("group", "tensor"), "fsdp", None, None),
        P(("group", "tensor"), "fsdp", None, None),
    )
    return jax.shard_map(
        on_device, mesh=mesh, in_specs=in_specs, out_specs=out_specs, check_vma=False
    )
```
